512 devices in a mesh: region: 64 (over y, z), sub: 8 (over x, core).
Axes of the slice: x: 4, y: 4, z: 16, core: 2. Of those that a mesh axis runs over, the one named last changes fastest.
Arguments:
- loads: bfloat16 [512, 32, 1024], P(('region', 'sub')), may hold values from -6 to 6
- index_blocks: int32 [512, 1024], P(('region', 'sub')), may hold values from 0 to 1023, each once within a row
- stiffness: bfloat16 [512, 1024, 1024], P(('region', 'sub')), as said below
- dirichlet: bfloat16 [512, 1024, 1024], P(('region', 'sub')), as said below
- modes: float32 [512, 6, 1024], P(('region', 'sub')), may hold values from -0.25 to 0.25
- coarse: float32 [3072, 3072], P(('region', 'sub')), as said below
Outputs:
- multiplier: float32 [512, 32, 1024], P(('region', 'sub'))
- projected: float32 [512, 32, 1024], P(('region', 'sub'))
The draws below stay inside these ranges and needn't reach their ends.
Inputs may be any that keep to these rules, and one draw needn't show every extreme that they name: Each row of index_blocks holds every number 0 to 1023 once. `stiffness`: each subdomain's matrix is symmetric. `dirichlet`: each subdomain's matrix is symmetric. `coarse`: symmetric.
All inputs are finite; a program needn't handle non-finite values.
Results may differ from the reference program's by a relative error of at most 0.0068.
Values sent between devices are 32-bit elements; how exact they have to be, the bound alone decides.
A program may use at most 64 MiB of HBM per device.

```python
import math
import jax
import jax.numpy as jnp
from jax import lax

B = 1024
LOADS = 32
MODES = 6
ITERS = 1
SUBDOMAINS = 512
N_REGION = 64
N_SUB = 8


def finish_block(raw, scales):
    size = raw.shape[0]
    eye = jnp.eye(size, dtype=jnp.float32)
    off_diag = (raw + raw.T) * (0.35 / math.sqrt(2.0 * size))
    matrix = off_diag * (1.0 - eye) + eye
    return matrix * scales[:, None] * scales[None, :]


def draw_stiffness(key, part):
    key = jax.random.fold_in(key, 11)

    def single(index):
        first, second = jax.random.split(jax.random.fold_in(key, index))
        raw = jax.random.normal(first, (B, B), jnp.float32)
        scales = jnp.exp(jax.random.uniform(second, (B,), jnp.float32, -0.5, 0.5))
        return finish_block(raw, scales).astype(jnp.bfloat16)
    return lax.map(single, jnp.arange(N_REGION * N_SUB))


def draw_dirichlet(key, part):
    key = jax.random.fold_in(key, 13)

    def single(index):
        first, second = jax.random.split(jax.random.fold_in(key, index))
        raw = jax.random.normal(first, (B, B), jnp.float32)
        scales = jnp.exp(jax.random.uniform(second, (B,), jnp.float32, -0.5, 0.5))
        return finish_block(raw, scales).astype(jnp.bfloat16)
    return lax.map(single, jnp.arange(N_REGION * N_SUB))


def draw_coarse(key, part):
    key = jax.random.fold_in(key, 17)
    first, second = jax.random.split(key)
    total = MODES * N_REGION * N_SUB
    raw = jax.random.normal(first, (total, total), jnp.float32)
    scales = jnp.exp(jax.random.uniform(second, (total,), jnp.float32, -0.15, 0.15))
    return finish_block(raw, scales)


def levels(stream_key, extent, pieces, smallest, largest):
    def one(axis_at, parts):
        steps = jax.random.uniform(jax.random.fold_in(jax.random.fold_in(stream_key, 6), axis_at), (parts,), jnp.float32, smallest / len(pieces), largest / len(pieces))
        return jnp.repeat(jnp.exp(steps), extent[axis_at] // parts).reshape((-1,) + (1,) * (len(extent) - axis_at - 1))

    loudness = one(*pieces[0])
    for cut in pieces[1:]:
        loudness = loudness * one(*cut)
    return loudness


def bell_draw(rng, dims, width, bound, pieces=(), held_as=jnp.bfloat16):
    loudness = levels(rng, dims, pieces, -0.22, 0.18) if pieces else 1.0
    entries = jax.random.normal(rng, dims, jnp.float32) * width * loudness
    return jnp.minimum(jnp.maximum(entries, -bound), bound).astype(held_as)


def setup_inputs(seed: int = 0) -> dict:
    splits = jax.random.split(jax.random.key(seed), 7)
    loads = bell_draw(splits[0], (SUBDOMAINS, LOADS, B), 1.0, 6.0, ((0, 512),))
    index_blocks = jax.vmap(lambda own: jax.random.permutation(own, B))(jax.random.split(splits[1], SUBDOMAINS)).reshape((SUBDOMAINS, B)).astype(jnp.int32)
    stiffness = draw_stiffness(jax.random.fold_in(splits[6], 71), 0)
    dirichlet = draw_dirichlet(jax.random.fold_in(splits[6], 71), 0)
    modes = bell_draw(splits[4], (SUBDOMAINS, MODES, B), (B // 2 + 96) ** -0.5, 0.25, ((0, 512),), jnp.float32)
    coarse = draw_coarse(jax.random.fold_in(splits[6], 71), 0)
    return dict(loads=loads, index_blocks=index_blocks, stiffness=stiffness, dirichlet=dirichlet, modes=modes, coarse=coarse)


def to_slots(matrix, vector, slot_map):
    local = jnp.zeros(vector.shape, jnp.float32).at[:, slot_map].set(vector)
    product = jnp.dot(local.astype(jnp.bfloat16), matrix, preferred_element_type=jnp.float32)
    return jnp.take(product, slot_map, axis=1)


def apply_all(matrices, vectors, index_blocks):
    return lax.map(lambda items: to_slots(items[0], items[1], items[2]), (matrices, vectors, index_blocks))


def jump_all(field):
    block = B // 8
    grid = field.reshape(N_REGION, N_SUB, LOADS, 8, block)
    next_sub = jnp.roll(grid, -1, axis=1)[:, :, :, 2:4]
    prev_sub = jnp.roll(grid, 1, axis=1)[:, :, :, 0:2]
    next_region = jnp.roll(grid, -1, axis=0)[:, :, :, 6:8]
    prev_region = jnp.roll(grid, 1, axis=0)[:, :, :, 4:6]
    partner = jnp.concatenate([next_sub, prev_sub, next_region, prev_region], axis=3)
    return field - partner.reshape(field.shape)


def project_all(field, modes, coarse):
    highest = lax.Precision.HIGHEST
    terms = jnp.einsum("skb,srb->skr", modes, field, precision=highest)
    values = jnp.dot(coarse, terms.reshape(-1, LOADS), precision=highest)
    values = values.reshape(terms.shape)
    rigid = jnp.einsum("skr,skb->srb", values, modes, precision=highest)
    return field - jump_all(rigid)


def reference(loads, index_blocks, stiffness, dirichlet, modes, coarse):
    def load_slots(items):
        product = jnp.dot(items[0], items[1], preferred_element_type=jnp.float32)
        return jnp.take(product, items[2], axis=1)

    residual = jump_all(lax.map(load_slots, (loads, stiffness, index_blocks)))
    multiplier = jnp.zeros(residual.shape, jnp.float32)
    projected = project_all(residual, modes, coarse)
    search = project_all(jump_all(apply_all(dirichlet, projected, index_blocks)), modes, coarse)
    rho = jnp.sum(residual * search, axis=(0, 2))
    direction = search
    for step in range(ITERS):
        image = jump_all(apply_all(stiffness, direction, index_blocks))
        alpha = rho / jnp.sum(direction * image, axis=(0, 2))
        multiplier = multiplier + alpha[None, :, None] * direction
        residual = residual - alpha[None, :, None] * image
        projected = project_all(residual, modes, coarse)
        if step + 1 < ITERS:
            search = project_all(jump_all(apply_all(dirichlet, projected, index_blocks)), modes, coarse)
            rho_next = jnp.sum(residual * search, axis=(0, 2))
            direction = search + (rho_next / rho)[None, :, None] * direction
            rho = rho_next
    return multiplier, projected
```

```python
import functools

import jax
import jax.numpy as jnp
import numpy as np
from jax import lax
from jax.experimental import pallas as pl
from jax.experimental.pallas import tpu as pltpu
from jax.sharding import PartitionSpec as P

MESH = pl.DeviceIdType.MESH
HIGHEST = lax.Precision.HIGHEST
F32 = jnp.float32
BF16 = jnp.bfloat16

WIDTH = 1024
CASES = 32
MODES = 6
QUARTER = WIDTH // 4
CHIPS_Z = 16
LANES = 128
GROUPS = LANES // CASES
NT = (((1,), (1,)), ((), ()))


def column_choice(nz, nu):
    choice = np.zeros((nz * nu * MODES, nu * LANES), np.float32)
    for z in range(nz):
        for u in range(nu):
            for i in range(MODES):
                lane = (i % GROUPS) * 32 + (i // GROUPS) * 16 + z
                choice[(z * nu + u) * MODES + i, u * LANES + lane] = 1.0
    return choice


def split3(x):
    hi = x.astype(BF16)
    rest = x - hi.astype(F32)
    mid = rest.astype(BF16)
    lo = (rest - mid.astype(F32)).astype(BF16)
    return jnp.concatenate([hi, mid, lo], axis=0)


def merge3(x):
    rows = x.shape[0] // 3
    return (x[:rows] + x[rows : 2 * rows]) + x[2 * rows :]


def kernel(
    ny, nz, nu,
    loads_in, index_in, stiff_in, dirich_in, modes_in, coarse_in, choice_in,
    mult_out, proj_out,
    loads_v, index_v, stiff_v, dirich_v, modes_v, coarse_v, choice_v,
    pick, pick_t, stiff_s, dirich_s,
    field, partner, shapes, other_shapes, weights,
    coarse_send, coarse_recv, xbuf, vsend, vrecv, nbuf,
    resid, projd, srch,
    in_sem, fsend, frecv, csend, crecv, gsend, grecv, psend, precv, nsend, nrecv,
):
    plane = ny * nu
    r = lax.axis_index("region")
    u = lax.axis_index("sub")
    y = lax.div(r, nz)
    z = lax.rem(r, nz)
    p = y * nu + u
    nr = ny * nz
    ahead_u, back_u = (r, lax.rem(u + 1, nu)), (r, lax.rem(u + nu - 1, nu))
    ahead_r, back_r = (lax.rem(r + 1, nr), u), (lax.rem(r + nr - 1, nr), u)

    def along_z(k):
        return (y * nz + lax.rem(z + k, nz), u)

    def in_plane(q):
        return (lax.div(q, nu) * nz + z, lax.rem(q, nu))

    loading = [
        pltpu.make_async_copy(a, b, in_sem.at[i])
        for i, (a, b) in enumerate(
            [
                (index_in, index_v),
                (loads_in, loads_v),
                (stiff_in, stiff_v),
                (modes_in, modes_v),
                (coarse_in, coarse_v),
                (choice_in, choice_v),
                (dirich_in, dirich_v),
            ]
        )
    ]
    for copy in loading:
        copy.start()

    barrier = pltpu.get_barrier_semaphore()

    def greet_z(k, _):
        pl.semaphore_signal(barrier, inc=1, device_id=along_z(k), device_id_type=MESH)
        return 0

    def greet_plane(k, _):
        pl.semaphore_signal(
            barrier, inc=1, device_id=in_plane(lax.rem(p + k, plane)), device_id_type=MESH
        )
        return 0

    lax.fori_loop(1, nz, greet_z, 0)
    lax.fori_loop(1, plane, greet_plane, 0)
    for there in (ahead_r, back_r):
        pl.semaphore_signal(barrier, inc=1, device_id=there, device_id_type=MESH)

    loading[0].wait()

    def build_pick(b, _):
        rows = pl.ds(pl.multiple_of(b * LANES, LANES), LANES)
        unknown = lax.broadcasted_iota(jnp.int32, (LANES, WIDTH), 0) + b * LANES
        pick[rows, :] = jnp.where(unknown == index_v[...], 1.0, 0.0).astype(BF16)
        return 0

    lax.fori_loop(0, WIDTH // LANES, build_pick, 0)

    loading[1].wait()
    loading[2].wait()
    product = jnp.dot(loads_v[...], stiff_v[...], preferred_element_type=F32)
    field[0] = merge3(jnp.dot(split3(product), pick[...], preferred_element_type=F32))

    loading[3].wait()
    shapes[...] = jnp.concatenate([modes_v[...], jnp.zeros((8 - MODES, WIDTH), F32)], axis=0)

    if nz < CHIPS_Z:
        xbuf[...] = jnp.zeros_like(xbuf)
    nbuf[...] = jnp.zeros_like(nbuf)

    pl.semaphore_wait(barrier, (nz - 1) + (plane - 1) + 2)

    def exchange(src, dst, at):
        routes = ((1, 0, back_u), (0, 1, ahead_u), (3, 2, back_r), (2, 3, ahead_r))
        copies = []
        for n, (have, want, there) in enumerate(routes):
            copies.append(
                pltpu.make_async_remote_copy(
                    src_ref=src.at[:, pl.ds(have * QUARTER, QUARTER)],
                    dst_ref=dst.at[:, pl.ds(want * QUARTER, QUARTER)],
                    send_sem=fsend.at[at, n],
                    recv_sem=frecv.at[at, n],
                    device_id=there,
                    device_id_type=MESH,
                )
            )
        for n in (2, 3, 0, 1):
            copies[n].start()
        return copies

    field_copies = [exchange(field.at[0], partner.at[0], 0)]
    shape_copies = exchange(shapes, other_shapes, 3)

    loading[4].wait()
    loading[5].wait()
    span = nz * nu * MODES
    own_rows = jnp.concatenate(
        [
            jnp.concatenate(
                [coarse_v[:, i * span : (i + 1) * span], jnp.zeros((8 - MODES, span), F32)], axis=0
            )
            for i in range(ny)
        ],
        axis=0,
    )
    sorted_rows = merge3(jnp.dot(split3(own_rows), choice_v[...], preferred_element_type=F32))
    row8 = lax.broadcasted_iota(jnp.int32, (8, LANES), 0)
    lane8 = lax.broadcasted_iota(jnp.int32, (8, LANES), 1)
    half8 = lax.rem(lax.div(lane8, 16), 2)
    group8 = lax.div(lane8, CASES)
    sums8 = jnp.where((row8 >= MODES) & (half8 == 1) & (group8 + GROUPS == row8), 1.0, 0.0)
    for q in range(plane):
        i, j = q // nu, q % nu
        coarse_send[q] = sorted_rows[8 * i : 8 * i + 8, LANES * j : LANES * (j + 1)] + sums8

    def send_coarse(k, _):
        q = lax.rem(p + k, plane)
        pltpu.make_async_remote_copy(
            src_ref=coarse_send.at[q],
            dst_ref=coarse_recv.at[p],
            send_sem=csend,
            recv_sem=crecv,
            device_id=in_plane(q),
            device_id_type=MESH,
        ).start()
        return 0

    lax.fori_loop(1, plane, send_coarse, 0)
    coarse_recv[pl.ds(p, 1)] = coarse_send[pl.ds(p, 1)]

    def wait_bytes(ref, sem):
        pltpu.make_async_copy(ref, ref, sem).wait()

    def build_pick_t(b, _):
        rows = pl.ds(pl.multiple_of(b * LANES, LANES), LANES)
        chunk = index_v[:, rows].astype(F32)
        column = jnp.broadcast_to(chunk, (LANES, LANES)).T
        unknown = lax.broadcasted_iota(jnp.int32, (LANES, WIDTH), 1).astype(F32)
        same = jnp.concatenate([column] * (WIDTH // LANES), axis=1) == unknown
        pick_t[rows, :] = jnp.where(same, 1.0, 0.0).astype(BF16)
        return 0

    lax.fori_loop(0, WIDTH // LANES, build_pick_t, 0)
    loading[6].wait()

    def to_slots(matrix, out, part):
        rows = pl.ds(part * QUARTER, QUARTER)
        half = jnp.dot(pick_t[rows, :], matrix[...], preferred_element_type=F32).astype(BF16)
        out[rows, :] = jnp.dot(half, pick[...], preferred_element_type=F32).astype(BF16)

    mine8 = lax.rem(row8, GROUPS) == group8

    def build_weights():
        for copy in shape_copies:
            copy.wait_recv()
        row = lax.broadcasted_iota(jnp.int32, (8, WIDTH), 0)
        block = lax.div(lax.broadcasted_iota(jnp.int32, (8, WIDTH), 1), QUARTER)
        for j in range(GROUPS):
            for h in range(2):
                at = (2 * j + h) * 8
                i = GROUPS * h + j
                if i < MODES:
                    weights[at : at + 8, :] = jnp.where(
                        row == 0,
                        shapes[i : i + 1, :],
                        jnp.where(row == block + 1, -other_shapes[i : i + 1, :], 0.0),
                    )
                else:
                    weights[at : at + 8, :] = jnp.zeros((8, WIDTH), F32)

    def coarse_terms(a, sums):
        terms = lax.dot_general(
            shapes[...], jnp.concatenate([a] * GROUPS, axis=0), NT,
            precision=HIGHEST, preferred_element_type=F32,
        )
        if sums is not None:
            row = lax.broadcasted_iota(jnp.int32, (8, 2 * LANES), 0)
            which = lax.div(lax.broadcasted_iota(jnp.int32, (8, 2 * LANES), 1), LANES)
            ones = jnp.where(row == which + MODES, 1.0, 0.0)
            narrow = jnp.concatenate(
                [sum(s[:, LANES * i : LANES * (i + 1)] for i in range(WIDTH // LANES)) for s in sums],
                axis=1,
            )
            terms = terms + lax.dot_general(
                ones, jnp.concatenate([narrow] * GROUPS, axis=0), NT,
                precision=HIGHEST, preferred_element_type=F32,
            )
        return jnp.where(mine8, terms, 0.0)

    def correction(at, a, sums, work):
        terms = coarse_terms(a, sums)
        for h in range(2):
            packed = jnp.sum(
                jnp.where(lax.div(row8, GROUPS) == h, terms, 0.0), axis=0, keepdims=True
            )
            xbuf[at, pl.ds(z, 1), h : h + 1, :] = packed[None]

        def send_terms(k, _):
            pltpu.make_async_remote_copy(
                src_ref=xbuf.at[at, z],
                dst_ref=xbuf.at[at, z],
                send_sem=gsend.at[at],
                recv_sem=grecv.at[at],
                device_id=along_z(k),
                device_id_type=MESH,
            ).start()
            return 0

        lax.fori_loop(1, nz, send_terms, 0)
        work[0]()
        if at == 0:
            wait_bytes(coarse_recv.at[pl.ds(0, plane - 1)], crecv)
        wait_bytes(xbuf.at[at, pl.ds(0, nz - 1)], grecv.at[at])
        line = jnp.concatenate([xbuf[at, :, 0, :], xbuf[at, :, 1, :]], axis=0)
        group = lax.div(lax.broadcasted_iota(jnp.int32, (2 * CHIPS_Z, LANES), 1), CASES)
        spread = []
        for j in range(GROUPS):
            own = jnp.where(group == j, line, 0.0)
            own = own + pltpu.roll(own, CASES, 1)
            spread.append(own + pltpu.roll(own, 2 * CASES, 1))
        part = jnp.dot(
            coarse_recv[...].reshape(plane * 8, LANES), jnp.concatenate(spread, axis=0),
            precision=HIGHEST, preferred_element_type=F32,
        ).reshape(plane, 8, LANES)
        part = jnp.where(mine8[None], part, 0.0)
        for h in range(2):
            vsend[at, :, h : h + 1, :] = jnp.sum(
                part[:, GROUPS * h : GROUPS * (h + 1), :], axis=1, keepdims=True
            )

        def send_part(k, _):
            q = lax.rem(p + k, plane)
            pltpu.make_async_remote_copy(
                src_ref=vsend.at[at, q],
                dst_ref=vrecv.at[at, p],
                send_sem=psend.at[at],
                recv_sem=precv.at[at],
                device_id=in_plane(q),
                device_id_type=MESH,
            ).start()
            return 0

        lax.fori_loop(1, plane, send_part, 0)
        vrecv[at, pl.ds(p, 1)] = vsend[at, pl.ds(p, 1)]
        work[1]()
        wait_bytes(vrecv.at[at, pl.ds(0, plane - 1)], precv.at[at])
        nbuf[at, 0] = jnp.sum(vrecv[at], axis=0)
        copies = []
        for n, there in enumerate((back_u, ahead_u, back_r, ahead_r)):
            copies.append(
                pltpu.make_async_remote_copy(
                    src_ref=nbuf.at[at, 0],
                    dst_ref=nbuf.at[at, n + 1],
                    send_sem=nsend.at[at, n],
                    recv_sem=nrecv.at[at, n],
                    device_id=there,
                    device_id_type=MESH,
                )
            )
        for copy in copies:
            copy.start()
        work[2]()
        for copy in copies:
            copy.wait_recv()
        halves = [nbuf[at, :, h, :] for h in range(2)]
        values = jnp.concatenate(
            [
                halves[h] if j == 0 else pltpu.roll(halves[h], LANES - CASES * j, 1)
                for j in range(GROUPS)
                for h in range(2)
            ],
            axis=0,
        ).T[:CASES]
        out = jnp.dot(values, weights[...], precision=HIGHEST, preferred_element_type=F32)
        return out, values, copies

    def finish(at, work):
        work()
        for copy in field_copies[at]:
            copy.wait_recv()
        return field[at] - partner[at]

    resid[...] = finish(0, lambda: to_slots(dirich_v, dirich_s, 0))
    correct, _, near0 = correction(
        0,
        resid[...],
        None,
        (
            lambda: to_slots(dirich_v, dirich_s, 1),
            lambda: to_slots(dirich_v, dirich_s, 2),
            lambda: (to_slots(dirich_v, dirich_s, 3), build_weights()),
        ),
    )
    projd[...] = resid[...] - correct

    field[1] = jnp.dot(projd[...].astype(BF16), dirich_s[...], preferred_element_type=F32)
    field_copies.append(exchange(field.at[1], partner.at[1], 1))
    srch[...] = finish(1, lambda: to_slots(stiff_v, stiff_s, 0))
    correct, _, near1 = correction(
        1,
        srch[...],
        None,
        tuple(functools.partial(to_slots, stiff_v, stiff_s, n) for n in (1, 2, 3)),
    )
    srch[...] = srch[...] - correct

    field[2] = jnp.dot(srch[...].astype(BF16), stiff_s[...], preferred_element_type=F32)
    field_copies.append(exchange(field.at[2], partner.at[2], 2))
    image = finish(2, lambda: None)
    correct, values, near2 = correction(
        2, image, (resid[...] * srch[...], srch[...] * image), (lambda: None,) * 3
    )
    at_rho = (2 * 2 + 1) * 8
    at_bend = (2 * 3 + 1) * 8
    alpha = values[:, at_rho : at_rho + 1] / values[:, at_bend : at_bend + 1]
    mult_out[0] = alpha * srch[...]
    proj_out[0] = projd[...] - alpha * (image - correct)

    for copies in field_copies + [shape_copies, near0, near1, near2]:
        for copy in copies:
            copy.wait_send()
    wait_bytes(coarse_send.at[pl.ds(0, plane - 1)], csend)
    for at in range(3):
        wait_bytes(xbuf.at[at, pl.ds(0, nz - 1)], gsend.at[at])
        wait_bytes(vsend.at[at, pl.ds(0, plane - 1)], psend.at[at])


def on_device(ny, nz, nu, loads, index_blocks, stiffness, dirichlet, modes, coarse):
    plane = ny * nu
    span = nz * nu * MODES
    choice = jnp.asarray(column_choice(nz, nu), BF16)
    dma = pltpu.SemaphoreType.DMA
    out = jax.ShapeDtypeStruct((1, CASES, WIDTH), F32)
    return pl.pallas_call(
        functools.partial(kernel, ny, nz, nu),
        out_shape=(out, out),
        in_specs=[pl.BlockSpec(memory_space=pl.ANY)] * 7,
        out_specs=[pl.BlockSpec(memory_space=pltpu.VMEM)] * 2,
        scratch_shapes=[
            pltpu.VMEM((CASES, WIDTH), BF16),
            pltpu.VMEM((1, WIDTH), jnp.int32),
            pltpu.VMEM((WIDTH, WIDTH), BF16),
            pltpu.VMEM((WIDTH, WIDTH), BF16),
            pltpu.VMEM((MODES, WIDTH), F32),
            pltpu.VMEM((MODES, ny * span), F32),
            pltpu.VMEM((span, nu * LANES), BF16),
            pltpu.VMEM((WIDTH, WIDTH), BF16),
            pltpu.VMEM((WIDTH, WIDTH), BF16),
            pltpu.VMEM((WIDTH, WIDTH), BF16),
            pltpu.VMEM((WIDTH, WIDTH), BF16),
            pltpu.VMEM((3, CASES, WIDTH), F32),
            pltpu.VMEM((3, CASES, WIDTH), F32),
            pltpu.VMEM((8, WIDTH), F32),
            pltpu.VMEM((8, WIDTH), F32),
            pltpu.VMEM((64, WIDTH), F32),
            pltpu.VMEM((plane, 8, LANES), F32),
            pltpu.VMEM((plane, 8, LANES), F32),
            pltpu.VMEM((3, CHIPS_Z, 2, LANES), F32),
            pltpu.VMEM((3, plane, 2, LANES), F32),
            pltpu.VMEM((3, plane, 2, LANES), F32),
            pltpu.VMEM((3, 8, 2, LANES), F32),
            pltpu.VMEM((CASES, WIDTH), F32),
            pltpu.VMEM((CASES, WIDTH), F32),
            pltpu.VMEM((CASES, WIDTH), F32),
            dma((7,)),
            dma((4, 4)),
            dma((4, 4)),
            dma,
            dma,
            dma((3,)),
            dma((3,)),
            dma((3,)),
            dma((3,)),
            dma((3, 4)),
            dma((3, 4)),
        ],
        compiler_params=pltpu.CompilerParams(
            collective_id=0, has_side_effects=True, vmem_limit_bytes=60 * 1024 * 1024
        ),
    )(
        loads[0], index_blocks, stiffness[0], dirichlet[0], modes[0], coarse, choice
    )


def solution(mesh):
    regions, nu = mesh.shape["region"], mesh.shape["sub"]
    nz = min(CHIPS_Z, regions // 2)
    both = ("region", "sub")
    return jax.shard_map(
        functools.partial(on_device, regions // nz, nz, nu),
        mesh=mesh,
        in_specs=(
            P(both, None, None),
            P(both, None),
            P(both, None, None),
            P(both, None, None),
            P(both, None, None),
            P(both, None),
        ),
        out_specs=(P(both, None, None), P(both, None, None)),
        check_vma=False,
    )
```

```python
import functools

import jax
import jax.numpy as jnp
from jax import lax
from jax.experimental import pallas as pl
from jax.experimental.pallas import tpu as pltpu
from jax.sharding import PartitionSpec as P

MESH = pl.DeviceIdType.MESH
HIGHEST = lax.Precision.HIGHEST
F32 = jnp.float32
BF16 = jnp.bfloat16

WIDTH = 1024
CASES = 32
MODES = 6
QUARTER = WIDTH // 4
CHIPS_Z = 16
LANES = 128
GROUPS = LANES // CASES
NT = (((1,), (1,)), ((), ()))


def split3(x):
    hi = x.astype(BF16)
    rest = x - hi.astype(F32)
    mid = rest.astype(BF16)
    lo = (rest - mid.astype(F32)).astype(BF16)
    return jnp.concatenate([hi, mid, lo], axis=0)


def merge3(x):
    rows = x.shape[0] // 3
    return (x[:rows] + x[rows : 2 * rows]) + x[2 * rows :]


def kernel(
    ny, nz, nu,
    loads_in, index_in, stiff_in, dirich_in, modes_in, coarse_in,
    mult_out, proj_out,
    loads_v, index_v, stiff_v, dirich_v, modes_v, coarse_v, choice,
    pick, pick_t, stiff_s, dirich_s,
    field, partner, shapes, other_shapes, to_ext, from_ext,
    coarse_send, coarse_recv, coarse_near, coarse_ext,
    xfirst, xbuf, vpart, vsend, vrecv, vrecv_r,
    resid, projd, srch,
    in_sem, fsend, frecv, csend, crecv, dsend, drecv, gsend, grecv, psend, precv, nsend, nrecv,
):
    plane = ny * nu
    r = lax.axis_index("region")
    u = lax.axis_index("sub")
    y = lax.div(r, nz)
    z = lax.rem(r, nz)
    p = y * nu + u
    nr = ny * nz
    ahead_u, back_u = (r, lax.rem(u + 1, nu)), (r, lax.rem(u + nu - 1, nu))
    ahead_r, back_r = (lax.rem(r + 1, nr), u), (lax.rem(r + nr - 1, nr), u)
    ahead_y, back_y = (lax.rem(r + nz, nr), u), (lax.rem(r + nr - nz, nr), u)

    def along_z(k):
        return (y * nz + lax.rem(z + k, nz), u)

    def in_plane(q, shift=0):
        return (lax.rem(lax.div(q, nu) * nz + z + (nr + shift), nr), lax.rem(q, nu))

    loading = [
        pltpu.make_async_copy(a, b, in_sem.at[i])
        for i, (a, b) in enumerate(
            [
                (index_in, index_v),
                (loads_in, loads_v),
                (stiff_in, stiff_v),
                (modes_in, modes_v),
                (coarse_in, coarse_v),
                (dirich_in, dirich_v),
            ]
        )
    ]
    for copy in loading:
        copy.start()

    barrier = pltpu.get_barrier_semaphore()

    def greet(there):
        pl.semaphore_signal(barrier, inc=1, device_id=there, device_id_type=MESH)

    def greet_z(k, _):
        greet(along_z(k))
        return 0

    def greet_plane(k, _):
        greet(in_plane(lax.rem(p + k, plane)))
        return 0

    def greet_near(k, _):
        q = lax.rem(p + k, plane)
        greet(in_plane(q, 1))
        greet(in_plane(q, -1))
        return 0

    lax.fori_loop(1, nz, greet_z, 0)
    lax.fori_loop(1, plane, greet_plane, 0)
    lax.fori_loop(0, plane, greet_near, 0)

    loading[0].wait()

    def build_pick(b, _):
        rows = pl.ds(pl.multiple_of(b * LANES, LANES), LANES)
        unknown = lax.broadcasted_iota(jnp.int32, (LANES, WIDTH), 0) + b * LANES
        pick[rows, :] = jnp.where(unknown == index_v[...], 1.0, 0.0).astype(BF16)
        return 0

    lax.fori_loop(0, WIDTH // LANES, build_pick, 0)

    loading[1].wait()
    loading[2].wait()
    product = jnp.dot(loads_v[...], stiff_v[...], preferred_element_type=F32)
    field[0] = merge3(jnp.dot(split3(product), pick[...], preferred_element_type=F32))

    loading[3].wait()
    shapes[...] = jnp.concatenate(
        [modes_v[:, 0, :], jnp.zeros((8 - MODES, WIDTH), F32)], axis=0
    )
    if nz < CHIPS_Z:
        xfirst[...] = jnp.zeros_like(xfirst)
        xbuf[...] = jnp.zeros_like(xbuf)

    pl.semaphore_wait(barrier, (nz - 1) + (plane - 1) + 2 * plane)

    def exchange(src, dst, at):
        routes = ((1, 0, back_u), (0, 1, ahead_u), (3, 2, back_r), (2, 3, ahead_r))
        copies = []
        for n, (have, want, there) in enumerate(routes):
            copies.append(
                pltpu.make_async_remote_copy(
                    src_ref=src.at[:, pl.ds(have * QUARTER, QUARTER)],
                    dst_ref=dst.at[:, pl.ds(want * QUARTER, QUARTER)],
                    send_sem=fsend.at[at, n],
                    recv_sem=frecv.at[at, n],
                    device_id=there,
                    device_id_type=MESH,
                )
            )
        for n in (2, 3, 0, 1):
            copies[n].start()
        return copies

    field_copies = [exchange(field.at[0], partner.at[0], 0)]
    shape_copies = exchange(shapes, other_shapes, 3)

    loading[4].wait()
    span = nz * nu * MODES
    place = lax.broadcasted_iota(jnp.int32, (1, nu * LANES), 1)
    mode = lax.rem(lax.div(place, 16), 2) * GROUPS + lax.rem(lax.div(place, 32), GROUPS)
    column = (lax.rem(place, 16) * nu + lax.div(place, LANES)) * MODES + mode
    column = jnp.where((mode < MODES) & (lax.rem(place, 16) < nz), column, -1)
    part = span // nz

    def build_choice(b, _):
        at = b * part
        if part % 16 == 0:
            at = pl.multiple_of(at, 16)
        row = lax.broadcasted_iota(jnp.int32, (part, nu * LANES), 0) + b * part
        choice[pl.ds(at, part), :] = jnp.where(row == column, 1.0, 0.0).astype(BF16)
        return 0

    lax.fori_loop(0, nz, build_choice, 0)
    own_rows = jnp.concatenate(
        [
            jnp.concatenate(
                [coarse_v[:, i * span : (i + 1) * span], jnp.zeros((8 - MODES, span), F32)], axis=0
            )
            for i in range(ny)
        ],
        axis=0,
    )
    sorted_rows = merge3(jnp.dot(split3(own_rows), choice[...], preferred_element_type=F32))
    row8 = lax.broadcasted_iota(jnp.int32, (8, LANES), 0)
    lane8 = lax.broadcasted_iota(jnp.int32, (8, LANES), 1)
    half8 = lax.rem(lax.div(lane8, 16), 2)
    group8 = lax.div(lane8, CASES)
    sums8 = jnp.where((row8 >= MODES) & (half8 == 1) & (group8 + GROUPS == row8), 1.0, 0.0)
    for q in range(plane):
        i, j = q // nu, q % nu
        coarse_send[q] = sorted_rows[8 * i : 8 * i + 8, LANES * j : LANES * (j + 1)] + sums8

    def send_coarse(k, _):
        q = lax.rem(p + k, plane)
        pltpu.make_async_remote_copy(
            src_ref=coarse_send.at[q],
            dst_ref=coarse_recv.at[p],
            send_sem=csend,
            recv_sem=crecv,
            device_id=in_plane(q),
            device_id_type=MESH,
        ).start()
        return 0

    lax.fori_loop(1, plane, send_coarse, 0)
    coarse_recv[pl.ds(p, 1)] = coarse_send[pl.ds(p, 1)]

    def wait_bytes(ref, sem):
        pltpu.make_async_copy(ref, ref, sem).wait()

    def build_pick_t(b, _):
        rows = pl.ds(pl.multiple_of(b * LANES, LANES), LANES)
        chunk = index_v[:, rows].astype(F32)
        column = jnp.broadcast_to(chunk, (LANES, LANES)).T
        unknown = lax.broadcasted_iota(jnp.int32, (LANES, WIDTH), 1).astype(F32)
        same = jnp.concatenate([column] * (WIDTH // LANES), axis=1) == unknown
        pick_t[rows, :] = jnp.where(same, 1.0, 0.0).astype(BF16)
        return 0

    lax.fori_loop(0, WIDTH // LANES, build_pick_t, 0)
    loading[5].wait()

    def to_slots(matrix, out, part):
        rows = pl.ds(part * QUARTER, QUARTER)
        half = jnp.dot(pick_t[rows, :], matrix[...], preferred_element_type=F32).astype(BF16)
        out[rows, :] = jnp.dot(half, pick[...], preferred_element_type=F32).astype(BF16)

    mine8 = lax.rem(row8, GROUPS) == group8
    vsend[...] = jnp.zeros_like(vsend)

    def build_weights():
        for copy in shape_copies:
            copy.wait_recv()
        block = lax.div(lax.broadcasted_iota(jnp.int32, (1, WIDTH), 1), QUARTER)
        nothing = jnp.zeros((1, WIDTH), F32)

        def mode_row(t, i):
            if t == 0:
                return shapes[i : i + 1, :]
            return jnp.where(block == t - 1, -other_shapes[i : i + 1, :], 0.0)

        rows_to = [nothing] * 32
        rows_from = [nothing] * 64
        for t in range(5):
            for i in range(MODES):
                h, j = divmod(i, GROUPS)
                row = mode_row(t, i)
                if t < 4:
                    rows_to[j * 8 + 2 * t + h] = row
                else:
                    rows_to[(2 + i % 2) * 8 + 2 * (i // 2) + 1] = row
                rows_from[j * 16 + (2 * t if t < 3 else 2 * t + 2) + h] = row
        for n in range(32):
            to_ext[n : n + 1, :] = rows_to[n]
        for n in range(64):
            from_ext[n : n + 1, :] = rows_from[n]

    def send_near_coarse():
        copies = []
        for n, there in enumerate((back_u, ahead_u, back_y, ahead_y)):
            copies.append(
                pltpu.make_async_remote_copy(
                    src_ref=coarse_recv,
                    dst_ref=coarse_near.at[n],
                    send_sem=dsend.at[n],
                    recv_sem=drecv.at[n],
                    device_id=there,
                    device_id_type=MESH,
                )
            )
        for copy in copies:
            copy.start()
        return copies

    def build_coarse_ext(copies):
        for copy in copies:
            copy.wait_recv()
        flat = (plane * 8, LANES)
        own = coarse_recv[...].reshape(flat)
        near = [coarse_near[n].reshape(flat) for n in range(4)]
        lane = lax.broadcasted_iota(jnp.int32, flat, 1)
        at_z = lax.rem(lane, 16)

        def roll(x, by):
            return pltpu.roll(x, by % LANES, 1) if by % LANES else x

        after = jnp.where(at_z == nz - 1, roll(near[2], nz - 1), roll(own, -1))
        before = jnp.where(at_z == 0, roll(near[3], 1 - nz), roll(own, 1))
        tiles = (own, near[0], near[1], after)
        for j in range(GROUPS):
            made = roll(tiles[0], -32 * j)
            for t in range(1, 4):
                made = jnp.where(lax.div(lane, 32) == t, roll(tiles[t], 32 * (t - j)), made)
            if j >= 2:
                for t in range(3):
                    h4, j4 = divmod(2 * t + j - 2, GROUPS)
                    moved = roll(before, 32 * t + 16 - 32 * j4 - 16 * h4)
                    made = jnp.where(lax.div(lane, 16) == 2 * t + 1, moved, made)
            coarse_ext[:, LANES * j : LANES * (j + 1)] = made

    def tiled(a):
        return jnp.concatenate([a] * GROUPS, axis=0)

    def spread(line):
        group = lax.div(lax.broadcasted_iota(jnp.int32, line.shape, 1), CASES)
        out = []
        for j in range(GROUPS):
            own = jnp.where(group == j, line, 0.0)
            own = own + pltpu.roll(own, CASES, 1)
            out.append(own + pltpu.roll(own, 2 * CASES, 1))
        return jnp.concatenate(out, axis=0)

    def send_line(at, ref):
        def send(k):
            pltpu.make_async_remote_copy(
                src_ref=ref.at[z],
                dst_ref=ref.at[z],
                send_sem=gsend.at[at],
                recv_sem=grecv.at[at],
                device_id=along_z(k),
                device_id_type=MESH,
            ).start()

        send(nz // 2)

        def both_ways(k, _):
            send(nz // 2 - k)
            send(nz // 2 + k)
            return 0

        lax.fori_loop(1, nz // 2, both_ways, 0)

    def first_terms(a):
        terms = lax.dot_general(
            shapes[...], tiled(a), NT, precision=HIGHEST, preferred_element_type=F32
        )
        terms = jnp.where(mine8, terms, 0.0)
        for h in range(2):
            packed = jnp.sum(
                jnp.where(lax.div(row8, GROUPS) == h, terms, 0.0), axis=0, keepdims=True
            )
            xfirst[pl.ds(z, 1), h : h + 1, :] = packed[None]
        send_line(0, xfirst)

    def first_product():
        wait_bytes(xfirst.at[pl.ds(0, nz - 1)], grecv.at[0])
        line = jnp.concatenate([xfirst[:, 0, :], xfirst[:, 1, :]], axis=0)
        return jnp.dot(
            coarse_recv[...].reshape(plane * 8, LANES), spread(line),
            precision=HIGHEST, preferred_element_type=F32,
        )

    def ext_terms(at, a, sums):
        terms = lax.dot_general(
            to_ext[...], tiled(a), NT, precision=HIGHEST, preferred_element_type=F32
        )
        if sums is not None:
            row = lax.broadcasted_iota(jnp.int32, (32, 2 * LANES), 0)
            which = lax.div(lax.broadcasted_iota(jnp.int32, (32, 2 * LANES), 1), LANES)
            ones = jnp.where(row == 8 * (which + 2) + 7, 1.0, 0.0)
            narrow = jnp.concatenate(
                [sum(s[:, LANES * i : LANES * (i + 1)] for i in range(WIDTH // LANES)) for s in sums],
                axis=1,
            )
            terms = terms + lax.dot_general(
                ones, tiled(narrow), NT, precision=HIGHEST, preferred_element_type=F32
            )
        packed = terms[:8]
        for j in range(1, GROUPS):
            packed = jnp.where(group8 == j, terms[8 * j : 8 * j + 8], packed)
        xbuf[at - 1, pl.ds(z, 1)] = packed[None]
        send_line(at, xbuf.at[at - 1])

    def ext_product(at):
        wait_bytes(xbuf.at[at - 1, pl.ds(0, nz - 1)], grecv.at[at])
        line = jnp.concatenate([xbuf[at - 1, :, n, :] for n in range(8)], axis=0)
        return jnp.dot(
            coarse_ext[...], spread(line), precision=HIGHEST, preferred_element_type=F32
        )

    def send_values(at, product):
        part = product.reshape(plane, 8, LANES)
        part = jnp.where(mine8[None], part, 0.0)
        for h in range(2):
            vpart[at, :, h : h + 1, :] = jnp.sum(
                part[:, GROUPS * h : GROUPS * (h + 1), :], axis=1, keepdims=True
            )

        def near(k, _):
            q = lax.rem(p + k, plane)
            for n, shift in enumerate((-1, 1)):
                pltpu.make_async_remote_copy(
                    src_ref=vpart.at[at, q],
                    dst_ref=vrecv_r.at[at, n, p],
                    send_sem=nsend.at[at, n],
                    recv_sem=nrecv.at[at, n],
                    device_id=in_plane(q, shift),
                    device_id_type=MESH,
                ).start()
            return 0

        lax.fori_loop(0, plane, near, 0)
        for i in range(ny):
            mine = vpart[at, nu * i : nu * (i + 1)]
            here = pl.ds(nu * i, nu)
            vsend[at, here, 0:2, :] = mine
            vsend[at, here, 2:4, :] = jnp.concatenate([mine[1:], mine[:1]], axis=0)
            vsend[at, here, 4:6, :] = jnp.concatenate([mine[nu - 1 :], mine[: nu - 1]], axis=0)

        def same(k, _):
            q = lax.rem(p + k, plane)
            pltpu.make_async_remote_copy(
                src_ref=vsend.at[at, q],
                dst_ref=vrecv.at[at, p],
                send_sem=psend.at[at],
                recv_sem=precv.at[at],
                device_id=in_plane(q),
                device_id_type=MESH,
            ).start()
            return 0

        lax.fori_loop(1, plane, same, 0)
        vrecv[at, pl.ds(p, 1)] = vsend[at, pl.ds(p, 1)]

    def rigid_jump(at):
        wait_bytes(vrecv.at[at, pl.ds(0, plane - 1)], precv.at[at])
        for n in range(2):
            wait_bytes(vrecv_r.at[at, n], nrecv.at[at, n])
        rows = jnp.concatenate(
            [jnp.sum(vrecv[at], axis=0)]
            + [jnp.sum(vrecv_r[at, n], axis=0) for n in range(2)]
            + [jnp.zeros((4, LANES), F32)],
            axis=0,
        )
        values = jnp.concatenate(
            [rows if j == 0 else pltpu.roll(rows, LANES - CASES * j, 1) for j in range(GROUPS)],
            axis=0,
        ).T[:CASES]
        out = jnp.dot(values, from_ext[...], precision=HIGHEST, preferred_element_type=F32)
        return out, values

    def jumped(at):
        for copy in field_copies[at]:
            copy.wait_recv()
        return field[at] - partner[at]

    to_slots(dirich_v, dirich_s, 0)
    resid[...] = jumped(0)
    first_terms(resid[...])
    to_slots(dirich_v, dirich_s, 1)
    to_slots(dirich_v, dirich_s, 2)
    wait_bytes(coarse_recv.at[pl.ds(0, plane - 1)], crecv)
    send_values(0, first_product())
    to_slots(dirich_v, dirich_s, 3)
    build_weights()
    correct, _ = rigid_jump(0)
    projd[...] = resid[...] - correct

    field[1] = jnp.dot(projd[...].astype(BF16), dirich_s[...], preferred_element_type=F32)
    ext_terms(1, field[1], None)
    field_copies.append(exchange(field.at[1], partner.at[1], 1))
    near_copies = send_near_coarse()
    to_slots(stiff_v, stiff_s, 0)
    to_slots(stiff_v, stiff_s, 1)
    build_coarse_ext(near_copies)
    send_values(1, ext_product(1))
    to_slots(stiff_v, stiff_s, 2)
    to_slots(stiff_v, stiff_s, 3)
    srch[...] = jumped(1)
    correct, _ = rigid_jump(1)
    srch[...] = srch[...] - correct

    field[2] = jnp.dot(srch[...].astype(BF16), stiff_s[...], preferred_element_type=F32)
    bend = field[2] * srch[...]
    ext_terms(2, field[2], (resid[...] * srch[...], bend + bend))
    field_copies.append(exchange(field.at[2], partner.at[2], 2))
    send_values(2, ext_product(2))
    image = jumped(2)
    correct, values = rigid_jump(2)
    alpha = values[:, 33:34] / values[:, 49:50]
    mult_out[0] = alpha * srch[...]
    proj_out[0] = projd[...] - alpha * (image - correct)

    for copies in field_copies + [shape_copies, near_copies]:
        for copy in copies:
            copy.wait_send()
    wait_bytes(coarse_send.at[pl.ds(0, plane - 1)], csend)
    wait_bytes(xfirst.at[pl.ds(0, nz - 1)], gsend.at[0])
    for at in range(3):
        if at:
            wait_bytes(xbuf.at[at - 1, pl.ds(0, nz - 1)], gsend.at[at])
        wait_bytes(vsend.at[at, pl.ds(0, plane - 1)], psend.at[at])
        for n in range(2):
            wait_bytes(vpart.at[at], nsend.at[at, n])


def on_device(ny, nz, nu, loads, index_blocks, stiffness, dirichlet, modes, coarse):
    plane = ny * nu
    span = nz * nu * MODES
    dma = pltpu.SemaphoreType.DMA
    out = jax.ShapeDtypeStruct((1, CASES, WIDTH), F32)
    return pl.pallas_call(
        functools.partial(kernel, ny, nz, nu),
        out_shape=(out, out),
        in_specs=[pl.BlockSpec(memory_space=pl.ANY)] * 6,
        out_specs=[pl.BlockSpec(memory_space=pltpu.VMEM)] * 2,
        scratch_shapes=[
            pltpu.VMEM((CASES, WIDTH), BF16),
            pltpu.VMEM((1, WIDTH), jnp.int32),
            pltpu.VMEM((WIDTH, WIDTH), BF16),
            pltpu.VMEM((WIDTH, WIDTH), BF16),
            pltpu.VMEM((MODES, 1, WIDTH), F32),
            pltpu.VMEM((MODES, ny * span), F32),
            pltpu.VMEM((span, nu * LANES), BF16),
            pltpu.VMEM((WIDTH, WIDTH), BF16),
            pltpu.VMEM((WIDTH, WIDTH), BF16),
            pltpu.VMEM((WIDTH, WIDTH), BF16),
            pltpu.VMEM((WIDTH, WIDTH), BF16),
            pltpu.VMEM((3, CASES, WIDTH), F32),
            pltpu.VMEM((3, CASES, WIDTH), F32),
            pltpu.VMEM((8, WIDTH), F32),
            pltpu.VMEM((8, WIDTH), F32),
            pltpu.VMEM((32, WIDTH), F32),
            pltpu.VMEM((64, WIDTH), F32),
            pltpu.VMEM((plane, 8, LANES), F32),
            pltpu.VMEM((plane, 8, LANES), F32),
            pltpu.VMEM((4, plane, 8, LANES), F32),
            pltpu.VMEM((plane * 8, GROUPS * LANES), F32),
            pltpu.VMEM((CHIPS_Z, 2, LANES), F32),
            pltpu.VMEM((2, CHIPS_Z, 8, LANES), F32),
            pltpu.VMEM((3, plane, 2, LANES), F32),
            pltpu.VMEM((3, plane, 8, LANES), F32),
            pltpu.VMEM((3, plane, 8, LANES), F32),
            pltpu.VMEM((3, 2, plane, 2, LANES), F32),
            pltpu.VMEM((CASES, WIDTH), F32),
            pltpu.VMEM((CASES, WIDTH), F32),
            pltpu.VMEM((CASES, WIDTH), F32),
            dma((6,)),
            dma((4, 4)),
            dma((4, 4)),
            dma,
            dma,
            dma((4,)),
            dma((4,)),
            dma((3,)),
            dma((3,)),
            dma((3,)),
            dma((3,)),
            dma((3, 2)),
            dma((3, 2)),
        ],
        compiler_params=pltpu.CompilerParams(
            collective_id=0, has_side_effects=True, vmem_limit_bytes=60 * 1024 * 1024
        ),
    )(
        loads[0],
        index_blocks,
        stiffness[0],
        dirichlet[0],
        jnp.transpose(modes, (1, 0, 2)),
        coarse,
    )


def solution(mesh):
    regions, nu = mesh.shape["region"], mesh.shape["sub"]
    nz = min(CHIPS_Z, regions // 2)
    both = ("region", "sub")
    return jax.shard_map(
        functools.partial(on_device, regions // nz, nz, nu),
        mesh=mesh,
        in_specs=(
            P(both, None, None),
            P(both, None),
            P(both, None, None),
            P(both, None, None),
            P(both, None, None),
            P(both, None),
        ),
        out_specs=(P(both, None, None), P(both, None, None)),
        check_vma=False,
    )
```

```python
import functools

import jax
import jax.numpy as jnp
from jax import lax
from jax.experimental import pallas as pl
from jax.experimental.pallas import tpu as pltpu
from jax.sharding import PartitionSpec as P

MESH = pl.DeviceIdType.MESH
HIGHEST = lax.Precision.HIGHEST
F32 = jnp.float32
BF16 = jnp.bfloat16

WIDTH = 1024
CASES = 32
MODES = 6
QUARTER = WIDTH // 4
CHIPS_Z = 16
LANES = 128
GROUPS = LANES // CASES
NT = (((1,), (1,)), ((), ()))


def split3(x):
    hi = x.astype(BF16)
    rest = x - hi.astype(F32)
    mid = rest.astype(BF16)
    lo = (rest - mid.astype(F32)).astype(BF16)
    return jnp.concatenate([hi, mid, lo], axis=0)


def merge3(x):
    rows = x.shape[0] // 3
    return (x[:rows] + x[rows : 2 * rows]) + x[2 * rows :]


def kernel(
    ny, nz, nu,
    loads_in, index_in, stiff_in, dirich_in, modes_in, coarse_in,
    srch_out, projd_out, step_out, alpha_out,
    loads_v, index_v, stiff_v, dirich_v, modes_v, coarse_v, choice,
    pick, pick_t, stiff_s, dirich_s,
    field, partner, shapes, other_shapes, to_ext,
    coarse_send, coarse_recv, coarse_near, coarse_ext,
    xfirst, xbuf, vpart, vsend, vrecv, vrecv_r,
    resid, projd, srch, moved, ratio, near_rows,
    in_sem, out_sem, fsend, frecv, csend, crecv, dsend, drecv, gsend, grecv, psend, precv, nsend, nrecv,
):
    plane = ny * nu
    r = lax.axis_index("region")
    u = lax.axis_index("sub")
    y = lax.div(r, nz)
    z = lax.rem(r, nz)
    p = y * nu + u
    nr = ny * nz
    ahead_u, back_u = (r, lax.rem(u + 1, nu)), (r, lax.rem(u + nu - 1, nu))
    ahead_r, back_r = (lax.rem(r + 1, nr), u), (lax.rem(r + nr - 1, nr), u)
    ahead_y, back_y = (lax.rem(r + nz, nr), u), (lax.rem(r + nr - nz, nr), u)

    def along_z(k):
        return (y * nz + lax.rem(z + k, nz), u)

    loading = [
        pltpu.make_async_copy(a, b, in_sem.at[i])
        for i, (a, b) in enumerate(
            [
                (index_in, index_v),
                (loads_in, loads_v),
                (stiff_in, stiff_v),
                (modes_in, modes_v),
                (coarse_in, coarse_v),
                (dirich_in, dirich_v),
            ]
        )
    ]
    for copy in loading:
        copy.start()

    barrier = pltpu.get_barrier_semaphore()

    def greet(there):
        pl.semaphore_signal(barrier, inc=1, device_id=there, device_id_type=MESH)

    def over_plane(visit):
        subs = [lax.rem(u + k, nu) for k in range(nu)]

        def row(k, _):
            at_y = lax.rem(y + lax.rem(k + ny // 2 - 1, ny - 1) + 1, ny)
            for at_u in subs:
                visit(at_y, at_u, False)
            return 0

        lax.fori_loop(0, ny - 1, row, 0)
        for k, at_u in enumerate(subs):
            visit(y, at_u, k == 0)

    def region_of(at_y, shift=0):
        if shift == 0:
            return at_y * nz + z
        return lax.rem(at_y * nz + z + (nr + shift), nr)

    def greet_z(k, _):
        greet(along_z(k))
        return 0

    def greet_plane(at_y, at_u, own):
        greet((region_of(at_y, 1), at_u))
        greet((region_of(at_y, -1), at_u))
        if not own:
            greet((region_of(at_y), at_u))

    lax.fori_loop(1, nz, greet_z, 0)
    over_plane(greet_plane)

    loading[0].wait()

    def build_pick(b, _):
        rows = pl.ds(pl.multiple_of(b * LANES, LANES), LANES)
        unknown = lax.broadcasted_iota(jnp.int32, (LANES, WIDTH), 0) + b * LANES
        pick[rows, :] = jnp.where(unknown == index_v[...], 1.0, 0.0).astype(BF16)
        return 0

    lax.fori_loop(0, WIDTH // LANES, build_pick, 0)

    loading[1].wait()
    loading[2].wait()
    product = jnp.dot(loads_v[...], stiff_v[...], preferred_element_type=F32)
    field[0] = merge3(jnp.dot(split3(product), pick[...], preferred_element_type=F32))

    loading[3].wait()
    shapes[...] = jnp.concatenate(
        [modes_v[:, 0, :], jnp.zeros((8 - MODES, WIDTH), F32)], axis=0
    )
    if nz < CHIPS_Z:
        xfirst[...] = jnp.zeros_like(xfirst)
        xbuf[...] = jnp.zeros_like(xbuf)

    pl.semaphore_wait(barrier, (nz - 1) + (plane - 1) + 2 * plane)

    def exchange(src, dst, at):
        routes = ((1, 0, back_u), (0, 1, ahead_u), (3, 2, back_r), (2, 3, ahead_r))
        copies = []
        for n, (have, want, there) in enumerate(routes):
            copies.append(
                pltpu.make_async_remote_copy(
                    src_ref=src.at[:, pl.ds(have * QUARTER, QUARTER)],
                    dst_ref=dst.at[:, pl.ds(want * QUARTER, QUARTER)],
                    send_sem=fsend.at[at, n],
                    recv_sem=frecv.at[at, n],
                    device_id=there,
                    device_id_type=MESH,
                )
            )
        for n in (2, 3, 0, 1):
            copies[n].start()
        return copies

    field_copies = [exchange(field.at[0], partner.at[0], 0)]
    shape_copies = exchange(shapes, other_shapes, 3)

    loading[4].wait()
    span = nz * nu * MODES
    place = lax.broadcasted_iota(jnp.int32, (1, nu * LANES), 1)
    mode = lax.rem(lax.div(place, 16), 2) * GROUPS + lax.rem(lax.div(place, 32), GROUPS)
    column = (lax.rem(place, 16) * nu + lax.div(place, LANES)) * MODES + mode
    column = jnp.where((mode < MODES) & (lax.rem(place, 16) < nz), column, -1)
    part = span // nz

    def build_choice(b, _):
        at = b * part
        if part % 16 == 0:
            at = pl.multiple_of(at, 16)
        row = lax.broadcasted_iota(jnp.int32, (part, nu * LANES), 0) + b * part
        choice[pl.ds(at, part), :] = jnp.where(row == column, 1.0, 0.0).astype(BF16)
        return 0

    lax.fori_loop(0, nz, build_choice, 0)
    own_rows = jnp.concatenate(
        [
            jnp.concatenate(
                [coarse_v[:, i * span : (i + 1) * span], jnp.zeros((8 - MODES, span), F32)], axis=0
            )
            for i in range(ny)
        ],
        axis=0,
    )
    sorted_rows = merge3(jnp.dot(split3(own_rows), choice[...], preferred_element_type=F32))
    row8 = lax.broadcasted_iota(jnp.int32, (8, LANES), 0)
    lane8 = lax.broadcasted_iota(jnp.int32, (8, LANES), 1)
    half8 = lax.rem(lax.div(lane8, 16), 2)
    group8 = lax.div(lane8, CASES)
    sums8 = jnp.where((row8 >= MODES) & (half8 == 1) & (group8 + GROUPS == row8), 1.0, 0.0)
    for q in range(plane):
        i, j = q // nu, q % nu
        coarse_send[q] = sorted_rows[8 * i : 8 * i + 8, LANES * j : LANES * (j + 1)] + sums8

    def send_coarse(at_y, at_u, own):
        if not own:
            pltpu.make_async_remote_copy(
                src_ref=coarse_send.at[at_y * nu + at_u],
                dst_ref=coarse_recv.at[p],
                send_sem=csend,
                recv_sem=crecv,
                device_id=(region_of(at_y), at_u),
                device_id_type=MESH,
            ).start()

    over_plane(send_coarse)
    coarse_recv[pl.ds(p, 1)] = coarse_send[pl.ds(p, 1)]

    def wait_bytes(ref, sem):
        pltpu.make_async_copy(ref, ref, sem).wait()

    def build_pick_t(b, _):
        rows = pl.ds(pl.multiple_of(b * LANES, LANES), LANES)
        chunk = index_v[:, rows].astype(F32)
        column = jnp.broadcast_to(chunk, (LANES, LANES)).T
        unknown = lax.broadcasted_iota(jnp.int32, (LANES, WIDTH), 1).astype(F32)
        same = jnp.concatenate([column] * (WIDTH // LANES), axis=1) == unknown
        pick_t[rows, :] = jnp.where(same, 1.0, 0.0).astype(BF16)
        return 0

    lax.fori_loop(0, WIDTH // LANES, build_pick_t, 0)
    loading[5].wait()

    def to_slots(matrix, out, part):
        rows = pl.ds(part * QUARTER, QUARTER)
        half = jnp.dot(pick_t[rows, :], matrix[...], preferred_element_type=F32).astype(BF16)
        out[rows, :] = jnp.dot(half, pick[...], preferred_element_type=F32).astype(BF16)

    mine8 = lax.rem(row8, GROUPS) == group8
    vsend[...] = jnp.zeros_like(vsend)

    def build_weights():
        for copy in shape_copies:
            copy.wait_recv()
        block = lax.div(lax.broadcasted_iota(jnp.int32, (1, WIDTH), 1), QUARTER)
        nothing = jnp.zeros((1, WIDTH), F32)

        def mode_row(t, i):
            if t == 0:
                return shapes[i : i + 1, :]
            return jnp.where(block == t - 1, -other_shapes[i : i + 1, :], 0.0)

        rows_to = [nothing] * 32
        for t in range(5):
            for i in range(MODES):
                h, j = divmod(i, GROUPS)
                row = mode_row(t, i)
                if t < 4:
                    rows_to[j * 8 + 2 * t + h] = row
                else:
                    rows_to[(2 + i % 2) * 8 + 2 * (i // 2) + 1] = row
        for n in range(32):
            to_ext[n : n + 1, :] = rows_to[n]

    def send_near_coarse():
        copies = []
        for n, there in enumerate((back_u, ahead_u, back_y, ahead_y)):
            copies.append(
                pltpu.make_async_remote_copy(
                    src_ref=coarse_recv,
                    dst_ref=coarse_near.at[n],
                    send_sem=dsend.at[n],
                    recv_sem=drecv.at[n],
                    device_id=there,
                    device_id_type=MESH,
                )
            )
        for copy in copies:
            copy.start()
        return copies

    def build_coarse_ext(copies):
        for copy in copies:
            copy.wait_recv()
        flat = (plane * 8, LANES)
        own = coarse_recv[...].reshape(flat)
        near = [coarse_near[n].reshape(flat) for n in range(4)]
        lane = lax.broadcasted_iota(jnp.int32, flat, 1)
        at_z = lax.rem(lane, 16)

        def roll(x, by):
            return pltpu.roll(x, by % LANES, 1) if by % LANES else x

        after = jnp.where(at_z == nz - 1, roll(near[2], nz - 1), roll(own, -1))
        before = jnp.where(at_z == 0, roll(near[3], 1 - nz), roll(own, 1))
        tiles = (own, near[0], near[1], after)
        for j in range(GROUPS):
            made = roll(tiles[0], -32 * j)
            for t in range(1, 4):
                made = jnp.where(lax.div(lane, 32) == t, roll(tiles[t], 32 * (t - j)), made)
            if j >= 2:
                for t in range(3):
                    h4, j4 = divmod(2 * t + j - 2, GROUPS)
                    moved = roll(before, 32 * t + 16 - 32 * j4 - 16 * h4)
                    made = jnp.where(lax.div(lane, 16) == 2 * t + 1, moved, made)
            coarse_ext[:, LANES * j : LANES * (j + 1)] = made

    def tiled(a):
        return jnp.concatenate([a] * GROUPS, axis=0)

    def spread(line):
        group = lax.div(lax.broadcasted_iota(jnp.int32, line.shape, 1), CASES)
        out = []
        for j in range(GROUPS):
            own = jnp.where(group == j, line, 0.0)
            own = own + pltpu.roll(own, CASES, 1)
            out.append(own + pltpu.roll(own, 2 * CASES, 1))
        return jnp.concatenate(out, axis=0)

    def send_line(at, ref):
        def send(k):
            pltpu.make_async_remote_copy(
                src_ref=ref.at[z],
                dst_ref=ref.at[z],
                send_sem=gsend.at[at],
                recv_sem=grecv.at[at],
                device_id=along_z(k),
                device_id_type=MESH,
            ).start()

        send(nz // 2)

        def both_ways(k, _):
            send(nz // 2 - k)
            send(nz // 2 + k)
            return 0

        lax.fori_loop(1, nz // 2, both_ways, 0)

    def first_terms(a):
        terms = lax.dot_general(
            shapes[...], tiled(a), NT, precision=HIGHEST, preferred_element_type=F32
        )
        terms = jnp.where(mine8, terms, 0.0)
        for h in range(2):
            packed = jnp.sum(
                jnp.where(lax.div(row8, GROUPS) == h, terms, 0.0), axis=0, keepdims=True
            )
            xfirst[pl.ds(z, 1), h : h + 1, :] = packed[None]
        send_line(0, xfirst)

    def first_product():
        wait_bytes(xfirst.at[pl.ds(0, nz - 1)], grecv.at[0])
        line = jnp.concatenate([xfirst[:, 0, :], xfirst[:, 1, :]], axis=0)
        return jnp.dot(
            coarse_recv[...].reshape(plane * 8, LANES), spread(line),
            precision=HIGHEST, preferred_element_type=F32,
        )

    def ext_of(rows, a):
        return lax.dot_general(
            rows, tiled(a), NT, precision=HIGHEST, preferred_element_type=F32
        )

    def inner(a, b):
        both = a * b
        narrow = sum(both[:, LANES * i : LANES * (i + 1)] for i in range(WIDTH // LANES))
        return ext_of(jnp.ones((8, LANES), F32), narrow)[:1]

    def exact(a, matrix):
        return merge3(jnp.dot(split3(a), matrix[...], preferred_element_type=F32))

    def send_ext(at, terms, sums):
        packed = terms[:8]
        for j in range(1, GROUPS):
            packed = jnp.where(group8 == j, terms[8 * j : 8 * j + 8], packed)
        if sums is not None:
            packed = jnp.where((row8 == 7) & (group8 == 2), sums[0], packed)
            packed = jnp.where((row8 == 7) & (group8 == 3), sums[1], packed)
        xbuf[at - 1, pl.ds(z, 1)] = packed[None]
        send_line(at, xbuf.at[at - 1])

    def ext_product(at):
        wait_bytes(xbuf.at[at - 1, pl.ds(0, nz - 1)], grecv.at[at])
        line = jnp.concatenate([xbuf[at - 1, :, n, :] for n in range(8)], axis=0)
        return jnp.dot(
            coarse_ext[...], spread(line), precision=HIGHEST, preferred_element_type=F32
        )

    def send_values(at, product):
        part = product.reshape(plane, 8, LANES)
        part = jnp.where(mine8[None], part, 0.0)
        for h in range(2):
            vpart[at, :, h : h + 1, :] = jnp.sum(
                part[:, GROUPS * h : GROUPS * (h + 1), :], axis=1, keepdims=True
            )

        def near(at_y, at_u, own):
            for n, shift in enumerate((-1, 1)):
                pltpu.make_async_remote_copy(
                    src_ref=vpart.at[at, at_y * nu + at_u],
                    dst_ref=vrecv_r.at[at, n, p],
                    send_sem=nsend.at[at, n],
                    recv_sem=nrecv.at[at, n],
                    device_id=(region_of(at_y, shift), at_u),
                    device_id_type=MESH,
                ).start()

        over_plane(near)
        for i in range(ny):
            mine = vpart[at, nu * i : nu * (i + 1)]
            here = pl.ds(nu * i, nu)
            vsend[at, here, 0:2, :] = mine
            vsend[at, here, 2:4, :] = jnp.concatenate([mine[1:], mine[:1]], axis=0)
            vsend[at, here, 4:6, :] = jnp.concatenate([mine[nu - 1 :], mine[: nu - 1]], axis=0)

        def same(at_y, at_u, own):
            if not own:
                pltpu.make_async_remote_copy(
                    src_ref=vsend.at[at, at_y * nu + at_u],
                    dst_ref=vrecv.at[at, p],
                    send_sem=psend.at[at],
                    recv_sem=precv.at[at],
                    device_id=(region_of(at_y), at_u),
                    device_id_type=MESH,
                ).start()

        over_plane(same)
        vrecv[at, pl.ds(p, 1)] = vsend[at, pl.ds(p, 1)]

    def values_here(at):
        wait_bytes(vrecv.at[at, pl.ds(0, plane - 1)], precv.at[at])
        for n in range(2):
            wait_bytes(vrecv_r.at[at, n], nrecv.at[at, n])
        near_rows[0:8, :] = jnp.sum(vrecv[at], axis=0)
        near_rows[6:8, :] = jnp.sum(vrecv_r[at, 0], axis=0)
        near_rows[8:10, :] = jnp.sum(vrecv_r[at, 1], axis=0)
        rows = near_rows[0:8, :]
        sums = rows[1:2]
        low, high = near_rows[8:9, :], near_rows[9:10, :]
        spare = group8 >= 2
        rows = jnp.where(spare & (row8 == 1), pltpu.roll(low, 2 * CASES, 1), rows)
        rows = jnp.where(spare & (row8 == 3), low, rows)
        rows = jnp.where(spare & (row8 == 5), pltpu.roll(high, 2 * CASES, 1), rows)
        rows = jnp.where(spare & (row8 == 7), 0.0, rows)
        return rows, sums

    def by_case(rows):
        return jnp.concatenate(
            [rows if j == 0 else pltpu.roll(rows, LANES - CASES * j, 1) for j in range(GROUPS)],
            axis=0,
        )

    def rigid_jump(rows):
        return jnp.dot(
            by_case(rows).T[:CASES], to_ext[...], precision=HIGHEST, preferred_element_type=F32
        )

    def times(bend, rows):
        return jnp.dot(bend, spread(rows), precision=HIGHEST, preferred_element_type=F32)

    def bending(moved_rows):
        return lax.dot_general(
            moved_rows, to_ext[...], NT, precision=HIGHEST, preferred_element_type=F32
        )

    def jumped(at):
        for copy in field_copies[at]:
            copy.wait_recv()
        return field[at] - partner[at]

    to_slots(dirich_v, dirich_s, 0)
    resid[...] = jumped(0)
    first_terms(resid[...])
    for n in (1, 2, 3):
        to_slots(dirich_v, dirich_s, n)
    build_weights()
    wait_bytes(coarse_recv.at[pl.ds(0, plane - 1)], crecv)
    send_values(0, first_product())
    moved[...] = exact(to_ext[...], dirich_s)
    bend = bending(moved[...])
    base = ext_of(moved[...], resid[...])
    resid_terms = ext_of(to_ext[...], resid[...])
    to_slots(stiff_v, stiff_s, 0)
    to_slots(stiff_v, stiff_s, 1)
    values, _ = values_here(0)

    send_ext(1, base - times(bend, values), None)
    projd[...] = resid[...] - rigid_jump(values)
    field[1] = jnp.dot(projd[...].astype(BF16), dirich_s[...], preferred_element_type=F32)
    field_copies.append(exchange(field.at[1], partner.at[1], 1))
    near_copies = send_near_coarse()
    to_slots(stiff_v, stiff_s, 2)
    to_slots(stiff_v, stiff_s, 3)
    build_coarse_ext(near_copies)
    send_values(1, ext_product(1))
    moved[...] = exact(to_ext[...], stiff_s)
    bend = bending(moved[...])
    srch[...] = jumped(1)
    base = ext_of(moved[...], srch[...])
    resid_inner = inner(resid[...], srch[...])
    image_inner = inner(srch[...], exact(srch[...], stiff_s))
    values, _ = values_here(1)

    terms = base - times(bend, values)
    each = spread(values)
    rho = resid_inner - jnp.sum(each * resid_terms, axis=0, keepdims=True)
    half = image_inner - jnp.sum(each * (base + terms), axis=0, keepdims=True)
    send_ext(2, terms, (rho, half + half))
    srch[...] = srch[...] - rigid_jump(values)
    field[2] = jnp.dot(srch[...].astype(BF16), stiff_s[...], preferred_element_type=F32)
    field_copies.append(exchange(field.at[2], partner.at[2], 2))
    done = [
        pltpu.make_async_copy(a, b, out_sem.at[n])
        for n, (a, b) in enumerate(
            [(srch, srch_out), (projd, projd_out), (resid, step_out), (ratio, alpha_out)]
        )
    ]
    done[0].start()
    done[1].start()
    send_values(2, ext_product(2))
    image = jumped(2)
    values, sums = values_here(2)
    quotient = pltpu.roll(sums / pltpu.roll(sums, LANES - CASES, 1), 2 * CASES, 1)
    ratio[...] = jnp.broadcast_to(quotient, (LANES, LANES)).T[:CASES]
    done[3].start()
    resid[...] = image - rigid_jump(values)
    done[2].start()
    for copy in done:
        copy.wait()

    for copies in field_copies + [shape_copies, near_copies]:
        for copy in copies:
            copy.wait_send()
    wait_bytes(coarse_send.at[pl.ds(0, plane - 1)], csend)
    wait_bytes(xfirst.at[pl.ds(0, nz - 1)], gsend.at[0])
    for at in range(3):
        if at:
            wait_bytes(xbuf.at[at - 1, pl.ds(0, nz - 1)], gsend.at[at])
        wait_bytes(vsend.at[at, pl.ds(0, plane - 1)], psend.at[at])
        for n in range(2):
            wait_bytes(vpart.at[at], nsend.at[at, n])


def on_device(ny, nz, nu, loads, index_blocks, stiffness, dirichlet, modes, coarse):
    plane = ny * nu
    span = nz * nu * MODES
    dma = pltpu.SemaphoreType.DMA
    out = jax.ShapeDtypeStruct((CASES, WIDTH), F32)
    search, projected, step, alpha = pl.pallas_call(
        functools.partial(kernel, ny, nz, nu),
        out_shape=(out, out, out, jax.ShapeDtypeStruct((CASES, LANES), F32)),
        in_specs=[pl.BlockSpec(memory_space=pl.ANY)] * 6,
        out_specs=[pl.BlockSpec(memory_space=pl.ANY)] * 4,
        scratch_shapes=[
            pltpu.VMEM((CASES, WIDTH), BF16),
            pltpu.VMEM((1, WIDTH), jnp.int32),
            pltpu.VMEM((WIDTH, WIDTH), BF16),
            pltpu.VMEM((WIDTH, WIDTH), BF16),
            pltpu.VMEM((MODES, 1, WIDTH), F32),
            pltpu.VMEM((MODES, ny * span), F32),
            pltpu.VMEM((span, nu * LANES), BF16),
            pltpu.VMEM((WIDTH, WIDTH), BF16),
            pltpu.VMEM((WIDTH, WIDTH), BF16),
            pltpu.VMEM((WIDTH, WIDTH), BF16),
            pltpu.VMEM((WIDTH, WIDTH), BF16),
            pltpu.VMEM((3, CASES, WIDTH), F32),
            pltpu.VMEM((3, CASES, WIDTH), F32),
            pltpu.VMEM((8, WIDTH), F32),
            pltpu.VMEM((8, WIDTH), F32),
            pltpu.VMEM((32, WIDTH), F32),
            pltpu.VMEM((plane, 8, LANES), F32),
            pltpu.VMEM((plane, 8, LANES), F32),
            pltpu.VMEM((4, plane, 8, LANES), F32),
            pltpu.VMEM((plane * 8, GROUPS * LANES), F32),
            pltpu.VMEM((CHIPS_Z, 2, LANES), F32),
            pltpu.VMEM((2, CHIPS_Z, 8, LANES), F32),
            pltpu.VMEM((3, plane, 2, LANES), F32),
            pltpu.VMEM((3, plane, 8, LANES), F32),
            pltpu.VMEM((3, plane, 8, LANES), F32),
            pltpu.VMEM((3, 2, plane, 2, LANES), F32),
            pltpu.VMEM((CASES, WIDTH), F32),
            pltpu.VMEM((CASES, WIDTH), F32),
            pltpu.VMEM((CASES, WIDTH), F32),
            pltpu.VMEM((32, WIDTH), F32),
            pltpu.VMEM((CASES, LANES), F32),
            pltpu.VMEM((16, LANES), F32),
            dma((6,)),
            dma((4,)),
            dma((4, 4)),
            dma((4, 4)),
            dma,
            dma,
            dma((4,)),
            dma((4,)),
            dma((3,)),
            dma((3,)),
            dma((3,)),
            dma((3,)),
            dma((3, 2)),
            dma((3, 2)),
        ],
        compiler_params=pltpu.CompilerParams(
            collective_id=0, has_side_effects=True, vmem_limit_bytes=60 * 1024 * 1024
        ),
    )(
        loads[0],
        index_blocks,
        stiffness[0],
        dirichlet[0],
        jnp.transpose(modes, (1, 0, 2)),
        coarse,
    )
    alpha = alpha[:, :1]
    return (alpha * search)[None], (projected - alpha * step)[None]


def solution(mesh):
    regions, nu = mesh.shape["region"], mesh.shape["sub"]
    nz = min(CHIPS_Z, regions // 2)
    both = ("region", "sub")
    return jax.shard_map(
        functools.partial(on_device, regions // nz, nz, nu),
        mesh=mesh,
        in_specs=(
            P(both, None, None),
            P(both, None),
            P(both, None, None),
            P(both, None, None),
            P(both, None, None),
            P(both, None),
        ),
        out_specs=(P(both, None, None), P(both, None, None)),
        check_vma=False,
    )
```

```python
import functools

import jax
import jax.numpy as jnp
from jax import lax
from jax.experimental import pallas as pl
from jax.experimental.pallas import tpu as pltpu
from jax.sharding import PartitionSpec as P

MESH = pl.DeviceIdType.MESH
HIGHEST = lax.Precision.HIGHEST
F32 = jnp.float32
BF16 = jnp.bfloat16

WIDTH = 1024
CASES = 32
MODES = 6
QUARTER = WIDTH // 4
CHIPS_Z = 16
LANES = 128
GROUPS = LANES // CASES
NN = (((1,), (0,)), ((), ()))
NT = (((1,), (1,)), ((), ()))


def split3(x):
    hi = x.astype(BF16)
    rest = x - hi.astype(F32)
    mid = rest.astype(BF16)
    lo = (rest - mid.astype(F32)).astype(BF16)
    return jnp.concatenate([hi, mid, lo], axis=0)


def product3(a, b, dims):
    def split(x):
        hi = x.astype(BF16)
        return hi, (x - hi.astype(F32)).astype(BF16)

    def dot(p, q):
        return lax.dot_general(p, q, dims, preferred_element_type=F32)

    (a_hi, a_lo), (b_hi, b_lo) = split(a), split(b)
    return dot(a_hi, b_hi) + (dot(a_hi, b_lo) + dot(a_lo, b_hi))


def merge3(x):
    rows = x.shape[0] // 3
    return (x[:rows] + x[rows : 2 * rows]) + x[2 * rows :]


def kernel(
    ny, nz, nu,
    loads_in, index_in, stiff_in, dirich_in, modes_in, coarse_in,
    srch_out, projd_out, step_out, alpha_out,
    loads_v, index_v, stiff_v, dirich_v, modes_v, coarse_v, choice,
    pick, pick_t, stiff_s, dirich_s,
    field, partner, shapes, other_shapes, to_ext,
    coarse_send, coarse_recv, coarse_near, coarse_ext,
    xfirst, xbuf, vpart, vsend, vrecv, vrecv_r,
    resid, projd, srch, moved, ratio, near_rows,
    in_sem, out_sem, fsend, frecv, csend, crecv, dsend, drecv, gsend, grecv, psend, precv, nsend, nrecv,
):
    plane = ny * nu
    r = lax.axis_index("region")
    u = lax.axis_index("sub")
    y = lax.div(r, nz)
    z = lax.rem(r, nz)
    p = y * nu + u
    nr = ny * nz
    ahead_u, back_u = (r, lax.rem(u + 1, nu)), (r, lax.rem(u + nu - 1, nu))
    ahead_r, back_r = (lax.rem(r + 1, nr), u), (lax.rem(r + nr - 1, nr), u)
    ahead_y, back_y = (lax.rem(r + nz, nr), u), (lax.rem(r + nr - nz, nr), u)

    def along_z(k):
        return (y * nz + lax.rem(z + k, nz), u)

    loading = [
        pltpu.make_async_copy(a, b, in_sem.at[i])
        for i, (a, b) in enumerate(
            [
                (index_in, index_v),
                (loads_in, loads_v),
                (stiff_in, stiff_v),
                (modes_in, modes_v),
                (coarse_in, coarse_v),
                (dirich_in, dirich_v),
            ]
        )
    ]
    for copy in loading:
        copy.start()

    barrier = pltpu.get_barrier_semaphore()

    def greet(there):
        pl.semaphore_signal(barrier, inc=1, device_id=there, device_id_type=MESH)

    def over_plane(visit):
        subs = [lax.rem(u + k, nu) for k in range(nu)]

        def row(k, _):
            at_y = lax.rem(y + lax.rem(k + ny // 2 - 1, ny - 1) + 1, ny)
            for at_u in subs:
                visit(at_y, at_u, False)
            return 0

        lax.fori_loop(0, ny - 1, row, 0)
        for k, at_u in enumerate(subs):
            visit(y, at_u, k == 0)

    def region_of(at_y, shift=0):
        if shift == 0:
            return at_y * nz + z
        return lax.rem(at_y * nz + z + (nr + shift), nr)

    def greet_z(k, _):
        greet(along_z(k))
        return 0

    def greet_plane(at_y, at_u, own):
        greet((region_of(at_y, 1), at_u))
        greet((region_of(at_y, -1), at_u))
        if not own:
            greet((region_of(at_y), at_u))

    lax.fori_loop(1, nz, greet_z, 0)
    over_plane(greet_plane)

    loading[0].wait()

    def build_pick(b, _):
        rows = pl.ds(pl.multiple_of(b * LANES, LANES), LANES)
        unknown = lax.broadcasted_iota(jnp.int32, (LANES, WIDTH), 0) + b * LANES
        pick[rows, :] = jnp.where(unknown == index_v[...], 1.0, 0.0).astype(BF16)
        return 0

    lax.fori_loop(0, WIDTH // LANES, build_pick, 0)

    loading[1].wait()
    loading[2].wait()
    product = jnp.dot(loads_v[...], stiff_v[...], preferred_element_type=F32)
    field[0] = merge3(jnp.dot(split3(product), pick[...], preferred_element_type=F32))

    loading[3].wait()
    shapes[...] = jnp.concatenate(
        [modes_v[:, 0, :], jnp.zeros((8 - MODES, WIDTH), F32)], axis=0
    )
    if nz < CHIPS_Z:
        xfirst[...] = jnp.zeros_like(xfirst)
        xbuf[...] = jnp.zeros_like(xbuf)

    pl.semaphore_wait(barrier, (nz - 1) + (plane - 1) + 2 * plane)

    def exchange(src, dst, at):
        routes = ((1, 0, back_u), (0, 1, ahead_u), (3, 2, back_r), (2, 3, ahead_r))
        copies = []
        for n, (have, want, there) in enumerate(routes):
            copies.append(
                pltpu.make_async_remote_copy(
                    src_ref=src.at[:, pl.ds(have * QUARTER, QUARTER)],
                    dst_ref=dst.at[:, pl.ds(want * QUARTER, QUARTER)],
                    send_sem=fsend.at[at, n],
                    recv_sem=frecv.at[at, n],
                    device_id=there,
                    device_id_type=MESH,
                )
            )
        for n in (2, 3, 0, 1):
            copies[n].start()
        return copies

    field_copies = [exchange(field.at[0], partner.at[0], 0)]
    shape_copies = exchange(shapes, other_shapes, 3)

    loading[4].wait()
    span = nz * nu * MODES
    place = lax.broadcasted_iota(jnp.int32, (1, nu * LANES), 1)
    mode = lax.rem(lax.div(place, 16), 2) * GROUPS + lax.rem(lax.div(place, 32), GROUPS)
    column = (lax.rem(place, 16) * nu + lax.div(place, LANES)) * MODES + mode
    column = jnp.where((mode < MODES) & (lax.rem(place, 16) < nz), column, -1)
    part = span // nz

    def build_choice(b, _):
        at = b * part
        if part % 16 == 0:
            at = pl.multiple_of(at, 16)
        row = lax.broadcasted_iota(jnp.int32, (part, nu * LANES), 0) + b * part
        choice[pl.ds(at, part), :] = jnp.where(row == column, 1.0, 0.0).astype(BF16)
        return 0

    lax.fori_loop(0, nz, build_choice, 0)
    own_rows = jnp.concatenate(
        [
            jnp.concatenate(
                [coarse_v[:, i * span : (i + 1) * span], jnp.zeros((8 - MODES, span), F32)], axis=0
            )
            for i in range(ny)
        ],
        axis=0,
    )
    sorted_rows = merge3(jnp.dot(split3(own_rows), choice[...], preferred_element_type=F32))
    row8 = lax.broadcasted_iota(jnp.int32, (8, LANES), 0)
    lane8 = lax.broadcasted_iota(jnp.int32, (8, LANES), 1)
    half8 = lax.rem(lax.div(lane8, 16), 2)
    group8 = lax.div(lane8, CASES)
    sums8 = jnp.where((row8 >= MODES) & (half8 == 1) & (group8 + GROUPS == row8), 1.0, 0.0)
    for q in range(plane):
        i, j = q // nu, q % nu
        coarse_send[q] = sorted_rows[8 * i : 8 * i + 8, LANES * j : LANES * (j + 1)] + sums8

    def send_coarse(at_y, at_u, own):
        if not own:
            pltpu.make_async_remote_copy(
                src_ref=coarse_send.at[at_y * nu + at_u],
                dst_ref=coarse_recv.at[p],
                send_sem=csend,
                recv_sem=crecv,
                device_id=(region_of(at_y), at_u),
                device_id_type=MESH,
            ).start()

    over_plane(send_coarse)
    coarse_recv[pl.ds(p, 1)] = coarse_send[pl.ds(p, 1)]

    def wait_bytes(ref, sem):
        pltpu.make_async_copy(ref, ref, sem).wait()

    def build_pick_t(b, _):
        rows = pl.ds(pl.multiple_of(b * LANES, LANES), LANES)
        chunk = index_v[:, rows].astype(F32)
        column = jnp.broadcast_to(chunk, (LANES, LANES)).T
        unknown = lax.broadcasted_iota(jnp.int32, (LANES, WIDTH), 1).astype(F32)
        same = jnp.concatenate([column] * (WIDTH // LANES), axis=1) == unknown
        pick_t[rows, :] = jnp.where(same, 1.0, 0.0).astype(BF16)
        return 0

    lax.fori_loop(0, WIDTH // LANES, build_pick_t, 0)
    loading[5].wait()

    def to_slots(matrix, out, part):
        rows = pl.ds(part * QUARTER, QUARTER)
        half = jnp.dot(pick_t[rows, :], matrix[...], preferred_element_type=F32).astype(BF16)
        out[rows, :] = jnp.dot(half, pick[...], preferred_element_type=F32).astype(BF16)

    mine8 = lax.rem(row8, GROUPS) == group8
    vsend[...] = jnp.zeros_like(vsend)

    def build_weights():
        for copy in shape_copies:
            copy.wait_recv()
        block = lax.div(lax.broadcasted_iota(jnp.int32, (1, WIDTH), 1), QUARTER)
        nothing = jnp.zeros((1, WIDTH), F32)

        def mode_row(t, i):
            if t == 0:
                return shapes[i : i + 1, :]
            return jnp.where(block == t - 1, -other_shapes[i : i + 1, :], 0.0)

        rows_to = [nothing] * 32
        for t in range(5):
            for i in range(MODES):
                h, j = divmod(i, GROUPS)
                row = mode_row(t, i)
                if t < 4:
                    rows_to[j * 8 + 2 * t + h] = row
                else:
                    rows_to[(2 + i % 2) * 8 + 2 * (i // 2) + 1] = row
        for n in range(32):
            to_ext[n : n + 1, :] = rows_to[n]

    def send_near_coarse():
        copies = []
        for n, there in enumerate((back_u, ahead_u, back_y, ahead_y)):
            copies.append(
                pltpu.make_async_remote_copy(
                    src_ref=coarse_recv,
                    dst_ref=coarse_near.at[n],
                    send_sem=dsend.at[n],
                    recv_sem=drecv.at[n],
                    device_id=there,
                    device_id_type=MESH,
                )
            )
        for copy in copies:
            copy.start()
        return copies

    def build_coarse_ext(copies):
        for copy in copies:
            copy.wait_recv()
        flat = (plane * 8, LANES)
        own = coarse_recv[...].reshape(flat)
        near = [coarse_near[n].reshape(flat) for n in range(4)]
        lane = lax.broadcasted_iota(jnp.int32, flat, 1)
        at_z = lax.rem(lane, 16)

        def roll(x, by):
            return pltpu.roll(x, by % LANES, 1) if by % LANES else x

        after = jnp.where(at_z == nz - 1, roll(near[2], nz - 1), roll(own, -1))
        before = jnp.where(at_z == 0, roll(near[3], 1 - nz), roll(own, 1))
        tiles = (own, near[0], near[1], after)
        for j in range(GROUPS):
            made = roll(tiles[0], -32 * j)
            for t in range(1, 4):
                made = jnp.where(lax.div(lane, 32) == t, roll(tiles[t], 32 * (t - j)), made)
            if j >= 2:
                for t in range(3):
                    h4, j4 = divmod(2 * t + j - 2, GROUPS)
                    moved = roll(before, 32 * t + 16 - 32 * j4 - 16 * h4)
                    made = jnp.where(lax.div(lane, 16) == 2 * t + 1, moved, made)
            coarse_ext[:, LANES * j : LANES * (j + 1)] = made

    def tiled(a):
        return jnp.concatenate([a] * GROUPS, axis=0)

    def spread(line):
        group = lax.div(lax.broadcasted_iota(jnp.int32, line.shape, 1), CASES)
        out = []
        for j in range(GROUPS):
            own = jnp.where(group == j, line, 0.0)
            own = own + pltpu.roll(own, CASES, 1)
            out.append(own + pltpu.roll(own, 2 * CASES, 1))
        return jnp.concatenate(out, axis=0)

    def send_line(at, ref):
        def send(k):
            pltpu.make_async_remote_copy(
                src_ref=ref.at[z],
                dst_ref=ref.at[z],
                send_sem=gsend.at[at],
                recv_sem=grecv.at[at],
                device_id=along_z(k),
                device_id_type=MESH,
            ).start()

        send(nz // 2)

        def both_ways(k, _):
            send(nz // 2 - k)
            send(nz // 2 + k)
            return 0

        lax.fori_loop(1, nz // 2, both_ways, 0)

    def first_terms(a):
        terms = product3(shapes[...], tiled(a), NT)
        terms = jnp.where(mine8, terms, 0.0)
        for h in range(2):
            packed = jnp.sum(
                jnp.where(lax.div(row8, GROUPS) == h, terms, 0.0), axis=0, keepdims=True
            )
            xfirst[pl.ds(z, 1), h : h + 1, :] = packed[None]
        send_line(0, xfirst)

    def first_product():
        wait_bytes(xfirst.at[pl.ds(0, nz - 1)], grecv.at[0])
        line = jnp.concatenate([xfirst[:, 0, :], xfirst[:, 1, :]], axis=0)
        return product3(coarse_recv[...].reshape(plane * 8, LANES), spread(line), NN)

    def ext_of(rows, a):
        return lax.dot_general(
            rows, tiled(a), NT, precision=HIGHEST, preferred_element_type=F32
        )

    def inner(a, b):
        both = a * b
        narrow = sum(both[:, LANES * i : LANES * (i + 1)] for i in range(WIDTH // LANES))
        return ext_of(jnp.ones((8, LANES), F32), narrow)[:1]

    def exact(a, matrix):
        return merge3(jnp.dot(split3(a), matrix[...], preferred_element_type=F32))

    def send_ext(at, terms, sums):
        packed = terms[:8]
        for j in range(1, GROUPS):
            packed = jnp.where(group8 == j, terms[8 * j : 8 * j + 8], packed)
        if sums is not None:
            packed = jnp.where((row8 == 7) & (group8 == 2), sums[0], packed)
            packed = jnp.where((row8 == 7) & (group8 == 3), sums[1], packed)
        xbuf[at - 1, pl.ds(z, 1)] = packed[None]
        send_line(at, xbuf.at[at - 1])

    def ext_product(at):
        wait_bytes(xbuf.at[at - 1, pl.ds(0, nz - 1)], grecv.at[at])
        line = jnp.concatenate([xbuf[at - 1, :, n, :] for n in range(8)], axis=0)
        return product3(coarse_ext[...], spread(line), NN)

    def send_values(at, product):
        part = product.reshape(plane, 8, LANES)
        part = jnp.where(mine8[None], part, 0.0)
        for h in range(2):
            vpart[at, :, h : h + 1, :] = jnp.sum(
                part[:, GROUPS * h : GROUPS * (h + 1), :], axis=1, keepdims=True
            )

        def near(at_y, at_u, own):
            for n, shift in enumerate((-1, 1)):
                pltpu.make_async_remote_copy(
                    src_ref=vpart.at[at, at_y * nu + at_u],
                    dst_ref=vrecv_r.at[at, n, p],
                    send_sem=nsend.at[at, n],
                    recv_sem=nrecv.at[at, n],
                    device_id=(region_of(at_y, shift), at_u),
                    device_id_type=MESH,
                ).start()

        over_plane(near)
        for i in range(ny):
            mine = vpart[at, nu * i : nu * (i + 1)]
            here = pl.ds(nu * i, nu)
            vsend[at, here, 0:2, :] = mine
            vsend[at, here, 2:4, :] = jnp.concatenate([mine[1:], mine[:1]], axis=0)
            vsend[at, here, 4:6, :] = jnp.concatenate([mine[nu - 1 :], mine[: nu - 1]], axis=0)

        def same(at_y, at_u, own):
            if not own:
                pltpu.make_async_remote_copy(
                    src_ref=vsend.at[at, at_y * nu + at_u],
                    dst_ref=vrecv.at[at, p],
                    send_sem=psend.at[at],
                    recv_sem=precv.at[at],
                    device_id=(region_of(at_y), at_u),
                    device_id_type=MESH,
                ).start()

        over_plane(same)
        vrecv[at, pl.ds(p, 1)] = vsend[at, pl.ds(p, 1)]

    def values_here(at):
        wait_bytes(vrecv.at[at, pl.ds(0, plane - 1)], precv.at[at])
        for n in range(2):
            wait_bytes(vrecv_r.at[at, n], nrecv.at[at, n])
        near_rows[0:8, :] = jnp.sum(vrecv[at], axis=0)
        near_rows[6:8, :] = jnp.sum(vrecv_r[at, 0], axis=0)
        near_rows[8:10, :] = jnp.sum(vrecv_r[at, 1], axis=0)
        rows = near_rows[0:8, :]
        sums = rows[1:2]
        low, high = near_rows[8:9, :], near_rows[9:10, :]
        spare = group8 >= 2
        rows = jnp.where(spare & (row8 == 1), pltpu.roll(low, 2 * CASES, 1), rows)
        rows = jnp.where(spare & (row8 == 3), low, rows)
        rows = jnp.where(spare & (row8 == 5), pltpu.roll(high, 2 * CASES, 1), rows)
        rows = jnp.where(spare & (row8 == 7), 0.0, rows)
        return rows, sums

    def by_case(rows):
        return jnp.concatenate(
            [rows if j == 0 else pltpu.roll(rows, LANES - CASES * j, 1) for j in range(GROUPS)],
            axis=0,
        )

    def rigid_jump(rows):
        return product3(by_case(rows).T[:CASES], to_ext[...], NN)

    def times(bend, rows):
        return product3(bend, spread(rows), NN)

    def bending(moved_rows):
        return lax.dot_general(
            moved_rows, to_ext[...], NT, precision=HIGHEST, preferred_element_type=F32
        )

    def jumped(at):
        for copy in field_copies[at]:
            copy.wait_recv()
        return field[at] - partner[at]

    to_slots(dirich_v, dirich_s, 0)
    resid[...] = jumped(0)
    first_terms(resid[...])
    for n in (1, 2, 3):
        to_slots(dirich_v, dirich_s, n)
    build_weights()
    wait_bytes(coarse_recv.at[pl.ds(0, plane - 1)], crecv)
    send_values(0, first_product())
    moved[...] = exact(to_ext[...], dirich_s)
    bend = bending(moved[...])
    base = ext_of(moved[...], resid[...])
    resid_terms = ext_of(to_ext[...], resid[...])
    to_slots(stiff_v, stiff_s, 0)
    to_slots(stiff_v, stiff_s, 1)
    values, _ = values_here(0)

    send_ext(1, base - times(bend, values), None)
    projd[...] = resid[...] - rigid_jump(values)
    field[1] = jnp.dot(projd[...].astype(BF16), dirich_s[...], preferred_element_type=F32)
    field_copies.append(exchange(field.at[1], partner.at[1], 1))
    near_copies = send_near_coarse()
    to_slots(stiff_v, stiff_s, 2)
    to_slots(stiff_v, stiff_s, 3)
    build_coarse_ext(near_copies)
    send_values(1, ext_product(1))
    moved[...] = exact(to_ext[...], stiff_s)
    bend = bending(moved[...])
    srch[...] = jumped(1)
    base = ext_of(moved[...], srch[...])
    resid_inner = inner(resid[...], srch[...])
    image_inner = inner(srch[...], exact(srch[...], stiff_s))
    values, _ = values_here(1)

    terms = base - times(bend, values)
    each = spread(values)
    rho = resid_inner - jnp.sum(each * resid_terms, axis=0, keepdims=True)
    half = image_inner - jnp.sum(each * (base + terms), axis=0, keepdims=True)
    send_ext(2, terms, (rho, half + half))
    srch[...] = srch[...] - rigid_jump(values)
    field[2] = jnp.dot(srch[...].astype(BF16), stiff_s[...], preferred_element_type=F32)
    field_copies.append(exchange(field.at[2], partner.at[2], 2))
    done = [
        pltpu.make_async_copy(a, b, out_sem.at[n])
        for n, (a, b) in enumerate(
            [(srch, srch_out), (projd, projd_out), (resid, step_out), (ratio, alpha_out)]
        )
    ]
    done[0].start()
    done[1].start()
    send_values(2, ext_product(2))
    image = jumped(2)
    values, sums = values_here(2)
    quotient = pltpu.roll(sums / pltpu.roll(sums, LANES - CASES, 1), 2 * CASES, 1)
    column = jnp.broadcast_to(quotient, (LANES, LANES)).T[:CASES]
    ratio[...] = jnp.concatenate([column] * (WIDTH // LANES), axis=1)
    done[3].start()
    resid[...] = image - rigid_jump(values)
    done[2].start()
    for copy in done:
        copy.wait()

    for copies in field_copies + [shape_copies, near_copies]:
        for copy in copies:
            copy.wait_send()
    wait_bytes(coarse_send.at[pl.ds(0, plane - 1)], csend)
    wait_bytes(xfirst.at[pl.ds(0, nz - 1)], gsend.at[0])
    for at in range(3):
        if at:
            wait_bytes(xbuf.at[at - 1, pl.ds(0, nz - 1)], gsend.at[at])
        wait_bytes(vsend.at[at, pl.ds(0, plane - 1)], psend.at[at])
        for n in range(2):
            wait_bytes(vpart.at[at], nsend.at[at, n])


def on_device(ny, nz, nu, loads, index_blocks, stiffness, dirichlet, modes, coarse):
    plane = ny * nu
    span = nz * nu * MODES
    dma = pltpu.SemaphoreType.DMA
    out = jax.ShapeDtypeStruct((CASES, WIDTH), F32)
    search, projected, step, alpha = pl.pallas_call(
        functools.partial(kernel, ny, nz, nu),
        out_shape=(pltpu.VMEM((CASES, WIDTH), F32),) * 4,
        in_specs=[pl.BlockSpec(memory_space=pl.ANY)] * 6,
        out_specs=[pl.BlockSpec(memory_space=pltpu.VMEM)] * 4,
        scratch_shapes=[
            pltpu.VMEM((CASES, WIDTH), BF16),
            pltpu.VMEM((1, WIDTH), jnp.int32),
            pltpu.VMEM((WIDTH, WIDTH), BF16),
            pltpu.VMEM((WIDTH, WIDTH), BF16),
            pltpu.VMEM((MODES, 1, WIDTH), F32),
            pltpu.VMEM((MODES, ny * span), F32),
            pltpu.VMEM((span, nu * LANES), BF16),
            pltpu.VMEM((WIDTH, WIDTH), BF16),
            pltpu.VMEM((WIDTH, WIDTH), BF16),
            pltpu.VMEM((WIDTH, WIDTH), BF16),
            pltpu.VMEM((WIDTH, WIDTH), BF16),
            pltpu.VMEM((3, CASES, WIDTH), F32),
            pltpu.VMEM((3, CASES, WIDTH), F32),
            pltpu.VMEM((8, WIDTH), F32),
            pltpu.VMEM((8, WIDTH), F32),
            pltpu.VMEM((32, WIDTH), F32),
            pltpu.VMEM((plane, 8, LANES), F32),
            pltpu.VMEM((plane, 8, LANES), F32),
            pltpu.VMEM((4, plane, 8, LANES), F32),
            pltpu.VMEM((plane * 8, GROUPS * LANES), F32),
            pltpu.VMEM((CHIPS_Z, 2, LANES), F32),
            pltpu.VMEM((2, CHIPS_Z, 8, LANES), F32),
            pltpu.VMEM((3, plane, 2, LANES), F32),
            pltpu.VMEM((3, plane, 8, LANES), F32),
            pltpu.VMEM((3, plane, 8, LANES), F32),
            pltpu.VMEM((3, 2, plane, 2, LANES), F32),
            pltpu.VMEM((CASES, WIDTH), F32),
            pltpu.VMEM((CASES, WIDTH), F32),
            pltpu.VMEM((CASES, WIDTH), F32),
            pltpu.VMEM((32, WIDTH), F32),
            pltpu.VMEM((CASES, WIDTH), F32),
            pltpu.VMEM((16, LANES), F32),
            dma((6,)),
            dma((4,)),
            dma((4, 4)),
            dma((4, 4)),
            dma,
            dma,
            dma((4,)),
            dma((4,)),
            dma((3,)),
            dma((3,)),
            dma((3,)),
            dma((3,)),
            dma((3, 2)),
            dma((3, 2)),
        ],
        compiler_params=pltpu.CompilerParams(
            collective_id=0, has_side_effects=True, vmem_limit_bytes=60 * 1024 * 1024
        ),
    )(
        loads[0],
        index_blocks,
        stiffness[0],
        dirichlet[0],
        jnp.transpose(modes, (1, 0, 2)),
        coarse,
    )
    return (alpha * search)[None], (projected - alpha * step)[None]


def solution(mesh):
    regions, nu = mesh.shape["region"], mesh.shape["sub"]
    nz = min(CHIPS_Z, regions // 2)
    both = ("region", "sub")
    return jax.shard_map(
        functools.partial(on_device, regions // nz, nz, nu),
        mesh=mesh,
        in_specs=(
            P(both, None, None),
            P(both, None),
            P(both, None, None),
            P(both, None, None),
            P(both, None, None),
            P(both, None),
        ),
        out_specs=(P(both, None, None), P(both, None, None)),
        check_vma=False,
    )
```

```python
import functools

import jax
import jax.numpy as jnp
from jax import lax
from jax.experimental import pallas as pl
from jax.experimental.pallas import tpu as pltpu
from jax.sharding import PartitionSpec as P

MESH = pl.DeviceIdType.MESH
HIGHEST = lax.Precision.HIGHEST
F32 = jnp.float32
BF16 = jnp.bfloat16

WIDTH = 1024
CASES = 32
MODES = 6
QUARTER = WIDTH // 4
CHIPS_Z = 16
LANES = 128
GROUPS = LANES // CASES
NN = (((1,), (0,)), ((), ()))
NT = (((1,), (1,)), ((), ()))


def split3(x):
    hi = x.astype(BF16)
    rest = x - hi.astype(F32)
    mid = rest.astype(BF16)
    lo = (rest - mid.astype(F32)).astype(BF16)
    return jnp.concatenate([hi, mid, lo], axis=0)


def product3(a, b, dims):
    def split(x):
        hi = x.astype(BF16)
        return hi, (x - hi.astype(F32)).astype(BF16)

    def dot(p, q):
        return lax.dot_general(p, q, dims, preferred_element_type=F32)

    (a_hi, a_lo), (b_hi, b_lo) = split(a), split(b)
    return dot(a_hi, b_hi) + (dot(a_hi, b_lo) + dot(a_lo, b_hi))


def merge3(x):
    rows = x.shape[0] // 3
    return (x[:rows] + x[rows : 2 * rows]) + x[2 * rows :]


def kernel(
    ny, nz, nu,
    loads_in, index_in, stiff_in, dirich_in, modes_in, coarse_in,
    srch_out, projd_out, step_out, alpha_out,
    loads_v, index_v, stiff_v, dirich_v, modes_v, coarse_v, choice,
    pick, pick_t, stiff_s, dirich_s,
    field, partner, shapes, other_shapes, to_ext,
    coarse_send, coarse_recv, coarse_near, coarse_ext,
    xfirst, xbuf, vpart, vsend, vrecv, vrecv_r,
    resid, projd, srch, moved, near_rows,
    in_sem, fsend, frecv, csend, crecv, dsend, drecv, gsend, grecv, psend, precv, nsend, nrecv,
):
    plane = ny * nu
    r = lax.axis_index("region")
    u = lax.axis_index("sub")
    y = lax.div(r, nz)
    z = lax.rem(r, nz)
    p = y * nu + u
    nr = ny * nz
    ahead_u, back_u = (r, lax.rem(u + 1, nu)), (r, lax.rem(u + nu - 1, nu))
    ahead_r, back_r = (lax.rem(r + 1, nr), u), (lax.rem(r + nr - 1, nr), u)
    ahead_y, back_y = (lax.rem(r + nz, nr), u), (lax.rem(r + nr - nz, nr), u)

    def along_z(k):
        return (y * nz + lax.rem(z + k, nz), u)

    loading = [
        pltpu.make_async_copy(a, b, in_sem.at[i])
        for i, (a, b) in enumerate(
            [
                (index_in, index_v),
                (loads_in, loads_v),
                (stiff_in, stiff_v),
                (modes_in, modes_v),
                (coarse_in, coarse_v),
                (dirich_in, dirich_v),
            ]
        )
    ]
    for copy in loading:
        copy.start()

    barrier = pltpu.get_barrier_semaphore()

    def greet(there):
        pl.semaphore_signal(barrier, inc=1, device_id=there, device_id_type=MESH)

    def over_plane(visit):
        subs = [lax.rem(u + k, nu) for k in range(nu)]

        def row(k, _):
            at_y = lax.rem(y + lax.rem(k + ny // 2 - 1, ny - 1) + 1, ny)
            for at_u in subs:
                visit(at_y, at_u, False)
            return 0

        lax.fori_loop(0, ny - 1, row, 0)
        for k, at_u in enumerate(subs):
            visit(y, at_u, k == 0)

    def region_of(at_y, shift=0):
        if shift == 0:
            return at_y * nz + z
        return lax.rem(at_y * nz + z + (nr + shift), nr)

    def greet_z(k, _):
        greet(along_z(k))
        return 0

    def greet_plane(at_y, at_u, own):
        greet((region_of(at_y, 1), at_u))
        greet((region_of(at_y, -1), at_u))
        if not own:
            greet((region_of(at_y), at_u))

    lax.fori_loop(1, nz, greet_z, 0)
    over_plane(greet_plane)

    loading[0].wait()

    def build_pick(b, _):
        rows = pl.ds(pl.multiple_of(b * LANES, LANES), LANES)
        unknown = lax.broadcasted_iota(jnp.int32, (LANES, WIDTH), 0) + b * LANES
        pick[rows, :] = jnp.where(unknown == index_v[...], 1.0, 0.0).astype(BF16)
        return 0

    lax.fori_loop(0, WIDTH // LANES, build_pick, 0)

    loading[1].wait()
    loading[2].wait()
    product = jnp.dot(loads_v[...], stiff_v[...], preferred_element_type=F32)
    field[0] = merge3(jnp.dot(split3(product), pick[...], preferred_element_type=F32))

    loading[3].wait()
    shapes[...] = jnp.concatenate(
        [modes_v[:, 0, :], jnp.zeros((8 - MODES, WIDTH), F32)], axis=0
    )
    if nz < CHIPS_Z:
        xfirst[...] = jnp.zeros_like(xfirst)
        xbuf[...] = jnp.zeros_like(xbuf)

    pl.semaphore_wait(barrier, (nz - 1) + (plane - 1) + 2 * plane)

    def exchange(src, dst, at):
        routes = ((1, 0, back_u), (0, 1, ahead_u), (3, 2, back_r), (2, 3, ahead_r))
        copies = []
        for n, (have, want, there) in enumerate(routes):
            copies.append(
                pltpu.make_async_remote_copy(
                    src_ref=src.at[:, pl.ds(have * QUARTER, QUARTER)],
                    dst_ref=dst.at[:, pl.ds(want * QUARTER, QUARTER)],
                    send_sem=fsend.at[at, n],
                    recv_sem=frecv.at[at, n],
                    device_id=there,
                    device_id_type=MESH,
                )
            )
        for n in (2, 3, 0, 1):
            copies[n].start()
        return copies

    field_copies = [exchange(field.at[0], partner.at[0], 0)]
    shape_copies = exchange(shapes, other_shapes, 3)

    loading[4].wait()
    span = nz * nu * MODES
    place = lax.broadcasted_iota(jnp.int32, (1, nu * LANES), 1)
    mode = lax.rem(lax.div(place, 16), 2) * GROUPS + lax.rem(lax.div(place, 32), GROUPS)
    column = (lax.rem(place, 16) * nu + lax.div(place, LANES)) * MODES + mode
    column = jnp.where((mode < MODES) & (lax.rem(place, 16) < nz), column, -1)
    part = span // nz

    def build_choice(b, _):
        at = b * part
        if part % 16 == 0:
            at = pl.multiple_of(at, 16)
        row = lax.broadcasted_iota(jnp.int32, (part, nu * LANES), 0) + b * part
        choice[pl.ds(at, part), :] = jnp.where(row == column, 1.0, 0.0).astype(BF16)
        return 0

    lax.fori_loop(0, nz, build_choice, 0)
    own_rows = jnp.concatenate(
        [
            jnp.concatenate(
                [coarse_v[:, i * span : (i + 1) * span], jnp.zeros((8 - MODES, span), F32)], axis=0
            )
            for i in range(ny)
        ],
        axis=0,
    )
    sorted_rows = merge3(jnp.dot(split3(own_rows), choice[...], preferred_element_type=F32))
    row8 = lax.broadcasted_iota(jnp.int32, (8, LANES), 0)
    lane8 = lax.broadcasted_iota(jnp.int32, (8, LANES), 1)
    half8 = lax.rem(lax.div(lane8, 16), 2)
    group8 = lax.div(lane8, CASES)
    sums8 = jnp.where((row8 >= MODES) & (half8 == 1) & (group8 + GROUPS == row8), 1.0, 0.0)
    for q in range(plane):
        i, j = q // nu, q % nu
        coarse_send[q] = sorted_rows[8 * i : 8 * i + 8, LANES * j : LANES * (j + 1)] + sums8

    def send_coarse(at_y, at_u, own):
        if not own:
            pltpu.make_async_remote_copy(
                src_ref=coarse_send.at[at_y * nu + at_u],
                dst_ref=coarse_recv.at[p],
                send_sem=csend,
                recv_sem=crecv,
                device_id=(region_of(at_y), at_u),
                device_id_type=MESH,
            ).start()

    over_plane(send_coarse)
    coarse_recv[pl.ds(p, 1)] = coarse_send[pl.ds(p, 1)]

    def wait_bytes(ref, sem):
        pltpu.make_async_copy(ref, ref, sem).wait()

    def build_pick_t(b, _):
        rows = pl.ds(pl.multiple_of(b * LANES, LANES), LANES)
        chunk = index_v[:, rows].astype(F32)
        column = jnp.broadcast_to(chunk, (LANES, LANES)).T
        unknown = lax.broadcasted_iota(jnp.int32, (LANES, WIDTH), 1).astype(F32)
        same = jnp.concatenate([column] * (WIDTH // LANES), axis=1) == unknown
        pick_t[rows, :] = jnp.where(same, 1.0, 0.0).astype(BF16)
        return 0

    lax.fori_loop(0, WIDTH // LANES, build_pick_t, 0)
    loading[5].wait()

    def to_slots(matrix, out, part):
        rows = pl.ds(part * QUARTER, QUARTER)
        half = jnp.dot(pick_t[rows, :], matrix[...], preferred_element_type=F32).astype(BF16)
        out[rows, :] = jnp.dot(half, pick[...], preferred_element_type=F32).astype(BF16)

    mine8 = lax.rem(row8, GROUPS) == group8
    vsend[...] = jnp.zeros_like(vsend)

    def build_weights():
        for copy in shape_copies:
            copy.wait_recv()
        block = lax.div(lax.broadcasted_iota(jnp.int32, (1, WIDTH), 1), QUARTER)
        nothing = jnp.zeros((1, WIDTH), F32)

        def mode_row(t, i):
            if t == 0:
                return shapes[i : i + 1, :]
            return jnp.where(block == t - 1, -other_shapes[i : i + 1, :], 0.0)

        rows_to = [nothing] * 32
        for t in range(5):
            for i in range(MODES):
                h, j = divmod(i, GROUPS)
                row = mode_row(t, i)
                if t < 4:
                    rows_to[j * 8 + 2 * t + h] = row
                else:
                    rows_to[(2 + i % 2) * 8 + 2 * (i // 2) + 1] = row
        for n in range(32):
            to_ext[n : n + 1, :] = rows_to[n]

    def send_near_coarse():
        copies = []
        for n, there in enumerate((back_u, ahead_u, back_y, ahead_y)):
            copies.append(
                pltpu.make_async_remote_copy(
                    src_ref=coarse_recv,
                    dst_ref=coarse_near.at[n],
                    send_sem=dsend.at[n],
                    recv_sem=drecv.at[n],
                    device_id=there,
                    device_id_type=MESH,
                )
            )
        for copy in copies:
            copy.start()
        return copies

    def build_coarse_ext(copies):
        for copy in copies:
            copy.wait_recv()
        flat = (plane * 8, LANES)
        own = coarse_recv[...].reshape(flat)
        near = [coarse_near[n].reshape(flat) for n in range(4)]
        lane = lax.broadcasted_iota(jnp.int32, flat, 1)
        at_z = lax.rem(lane, 16)

        def roll(x, by):
            return pltpu.roll(x, by % LANES, 1) if by % LANES else x

        after = jnp.where(at_z == nz - 1, roll(near[2], nz - 1), roll(own, -1))
        before = jnp.where(at_z == 0, roll(near[3], 1 - nz), roll(own, 1))
        tiles = (own, near[0], near[1], after)
        for j in range(GROUPS):
            made = roll(tiles[0], -32 * j)
            for t in range(1, 4):
                made = jnp.where(lax.div(lane, 32) == t, roll(tiles[t], 32 * (t - j)), made)
            if j >= 2:
                for t in range(3):
                    h4, j4 = divmod(2 * t + j - 2, GROUPS)
                    moved = roll(before, 32 * t + 16 - 32 * j4 - 16 * h4)
                    made = jnp.where(lax.div(lane, 16) == 2 * t + 1, moved, made)
            coarse_ext[:, LANES * j : LANES * (j + 1)] = made

    def tiled(a):
        return jnp.concatenate([a] * GROUPS, axis=0)

    def spread(line):
        group = lax.div(lax.broadcasted_iota(jnp.int32, line.shape, 1), CASES)
        out = []
        for j in range(GROUPS):
            own = jnp.where(group == j, line, 0.0)
            own = own + pltpu.roll(own, CASES, 1)
            out.append(own + pltpu.roll(own, 2 * CASES, 1))
        return jnp.concatenate(out, axis=0)

    def send_line(at, ref):
        def send(k):
            pltpu.make_async_remote_copy(
                src_ref=ref.at[z],
                dst_ref=ref.at[z],
                send_sem=gsend.at[at],
                recv_sem=grecv.at[at],
                device_id=along_z(k),
                device_id_type=MESH,
            ).start()

        send(nz // 2)

        def both_ways(k, _):
            send(nz // 2 - k)
            send(nz // 2 + k)
            return 0

        lax.fori_loop(1, nz // 2, both_ways, 0)

    def first_terms(a):
        terms = product3(shapes[...], tiled(a), NT)
        terms = jnp.where(mine8, terms, 0.0)
        for h in range(2):
            packed = jnp.sum(
                jnp.where(lax.div(row8, GROUPS) == h, terms, 0.0), axis=0, keepdims=True
            )
            xfirst[pl.ds(z, 1), h : h + 1, :] = packed[None]
        send_line(0, xfirst)

    def first_product():
        wait_bytes(xfirst.at[pl.ds(0, nz - 1)], grecv.at[0])
        line = jnp.concatenate([xfirst[:, 0, :], xfirst[:, 1, :]], axis=0)
        return product3(coarse_recv[...].reshape(plane * 8, LANES), spread(line), NN)

    def ext_of(rows, a):
        return lax.dot_general(
            rows, tiled(a), NT, precision=HIGHEST, preferred_element_type=F32
        )

    def inner(a, b):
        both = a * b
        narrow = sum(both[:, LANES * i : LANES * (i + 1)] for i in range(WIDTH // LANES))
        return ext_of(jnp.ones((8, LANES), F32), narrow)[:1]

    def exact(a, matrix):
        return merge3(jnp.dot(split3(a), matrix[...], preferred_element_type=F32))

    def send_ext(at, terms, sums):
        packed = terms[:8]
        for j in range(1, GROUPS):
            packed = jnp.where(group8 == j, terms[8 * j : 8 * j + 8], packed)
        if sums is not None:
            packed = jnp.where((row8 == 7) & (group8 == 2), sums[0], packed)
            packed = jnp.where((row8 == 7) & (group8 == 3), sums[1], packed)
        xbuf[at - 1, pl.ds(z, 1)] = packed[None]
        send_line(at, xbuf.at[at - 1])

    def ext_product(at):
        wait_bytes(xbuf.at[at - 1, pl.ds(0, nz - 1)], grecv.at[at])
        line = jnp.concatenate([xbuf[at - 1, :, n, :] for n in range(8)], axis=0)
        return product3(coarse_ext[...], spread(line), NN)

    def send_values(at, product):
        part = product.reshape(plane, 8, LANES)
        part = jnp.where(mine8[None], part, 0.0)
        for h in range(2):
            vpart[at, :, h : h + 1, :] = jnp.sum(
                part[:, GROUPS * h : GROUPS * (h + 1), :], axis=1, keepdims=True
            )

        def near(at_y, at_u, own):
            for n, shift in enumerate((-1, 1)):
                pltpu.make_async_remote_copy(
                    src_ref=vpart.at[at, at_y * nu + at_u],
                    dst_ref=vrecv_r.at[at, n, p],
                    send_sem=nsend.at[at, n],
                    recv_sem=nrecv.at[at, n],
                    device_id=(region_of(at_y, shift), at_u),
                    device_id_type=MESH,
                ).start()

        over_plane(near)
        for i in range(ny):
            mine = vpart[at, nu * i : nu * (i + 1)]
            here = pl.ds(nu * i, nu)
            vsend[at, here, 0:2, :] = mine
            vsend[at, here, 2:4, :] = jnp.concatenate([mine[1:], mine[:1]], axis=0)
            vsend[at, here, 4:6, :] = jnp.concatenate([mine[nu - 1 :], mine[: nu - 1]], axis=0)

        def same(at_y, at_u, own):
            if not own:
                pltpu.make_async_remote_copy(
                    src_ref=vsend.at[at, at_y * nu + at_u],
                    dst_ref=vrecv.at[at, p],
                    send_sem=psend.at[at],
                    recv_sem=precv.at[at],
                    device_id=(region_of(at_y), at_u),
                    device_id_type=MESH,
                ).start()

        over_plane(same)
        vrecv[at, pl.ds(p, 1)] = vsend[at, pl.ds(p, 1)]

    def values_here(at):
        wait_bytes(vrecv.at[at, pl.ds(0, plane - 1)], precv.at[at])
        for n in range(2):
            wait_bytes(vrecv_r.at[at, n], nrecv.at[at, n])
        near_rows[0:8, :] = jnp.sum(vrecv[at], axis=0)
        near_rows[6:8, :] = jnp.sum(vrecv_r[at, 0], axis=0)
        near_rows[8:10, :] = jnp.sum(vrecv_r[at, 1], axis=0)
        rows = near_rows[0:8, :]
        sums = rows[1:2]
        low, high = near_rows[8:9, :], near_rows[9:10, :]
        spare = group8 >= 2
        rows = jnp.where(spare & (row8 == 1), pltpu.roll(low, 2 * CASES, 1), rows)
        rows = jnp.where(spare & (row8 == 3), low, rows)
        rows = jnp.where(spare & (row8 == 5), pltpu.roll(high, 2 * CASES, 1), rows)
        rows = jnp.where(spare & (row8 == 7), 0.0, rows)
        return rows, sums

    def by_case(rows):
        return jnp.concatenate(
            [rows if j == 0 else pltpu.roll(rows, LANES - CASES * j, 1) for j in range(GROUPS)],
            axis=0,
        )

    def rigid_jump(rows):
        return product3(by_case(rows).T[:CASES], to_ext[...], NN)

    def times(bend, rows):
        return product3(bend, spread(rows), NN)

    def bending(moved_rows):
        return lax.dot_general(
            moved_rows, to_ext[...], NT, precision=HIGHEST, preferred_element_type=F32
        )

    def jumped(at):
        for copy in field_copies[at]:
            copy.wait_recv()
        return field[at] - partner[at]

    to_slots(dirich_v, dirich_s, 0)
    resid[...] = jumped(0)
    first_terms(resid[...])
    for n in (1, 2, 3):
        to_slots(dirich_v, dirich_s, n)
    build_weights()
    wait_bytes(coarse_recv.at[pl.ds(0, plane - 1)], crecv)
    send_values(0, first_product())
    moved[...] = exact(to_ext[...], dirich_s)
    bend = bending(moved[...])
    base = ext_of(moved[...], resid[...])
    resid_terms = ext_of(to_ext[...], resid[...])
    to_slots(stiff_v, stiff_s, 0)
    to_slots(stiff_v, stiff_s, 1)
    values, _ = values_here(0)

    send_ext(1, base - times(bend, values), None)
    projd[...] = resid[...] - rigid_jump(values)
    field[1] = jnp.dot(projd[...].astype(BF16), dirich_s[...], preferred_element_type=F32)
    field_copies.append(exchange(field.at[1], partner.at[1], 1))
    near_copies = send_near_coarse()
    to_slots(stiff_v, stiff_s, 2)
    to_slots(stiff_v, stiff_s, 3)
    build_coarse_ext(near_copies)
    send_values(1, ext_product(1))
    moved[...] = exact(to_ext[...], stiff_s)
    bend = bending(moved[...])
    srch[...] = jumped(1)
    base = ext_of(moved[...], srch[...])
    resid_inner = inner(resid[...], srch[...])
    image_inner = inner(srch[...], exact(srch[...], stiff_s))
    values, _ = values_here(1)

    terms = base - times(bend, values)
    each = spread(values)
    rho = resid_inner - jnp.sum(each * resid_terms, axis=0, keepdims=True)
    half = image_inner - jnp.sum(each * (base + terms), axis=0, keepdims=True)
    send_ext(2, terms, (rho, half + half))
    srch[...] = srch[...] - rigid_jump(values)
    field[2] = jnp.dot(srch[...].astype(BF16), stiff_s[...], preferred_element_type=F32)
    field_copies.append(exchange(field.at[2], partner.at[2], 2))
    srch_out[...] = srch[...]
    projd_out[...] = projd[...]
    send_values(2, ext_product(2))
    for copies in field_copies + [shape_copies, near_copies]:
        for copy in copies:
            copy.wait_send()
    wait_bytes(coarse_send.at[pl.ds(0, plane - 1)], csend)
    wait_bytes(xfirst.at[pl.ds(0, nz - 1)], gsend.at[0])
    for at in range(2):
        wait_bytes(xbuf.at[at, pl.ds(0, nz - 1)], gsend.at[at + 1])

    def sent_values(at):
        wait_bytes(vsend.at[at, pl.ds(0, plane - 1)], psend.at[at])
        for n in range(2):
            wait_bytes(vpart.at[at], nsend.at[at, n])

    sent_values(0)
    sent_values(1)
    image = jumped(2)
    values, sums = values_here(2)
    quotient = pltpu.roll(sums / pltpu.roll(sums, LANES - CASES, 1), 2 * CASES, 1)
    column = jnp.broadcast_to(quotient, (LANES, LANES)).T[:CASES]
    alpha_out[...] = jnp.concatenate([column] * (WIDTH // LANES), axis=1)
    step_out[...] = image - rigid_jump(values)
    sent_values(2)


def on_device(ny, nz, nu, loads, index_blocks, stiffness, dirichlet, modes, coarse):
    plane = ny * nu
    span = nz * nu * MODES
    dma = pltpu.SemaphoreType.DMA
    out = jax.ShapeDtypeStruct((CASES, WIDTH), F32)
    search, projected, step, alpha = pl.pallas_call(
        functools.partial(kernel, ny, nz, nu),
        out_shape=(pltpu.VMEM((CASES, WIDTH), F32),) * 4,
        in_specs=[pl.BlockSpec(memory_space=pl.ANY)] * 6,
        out_specs=[pl.BlockSpec(memory_space=pltpu.VMEM)] * 4,
        scratch_shapes=[
            pltpu.VMEM((CASES, WIDTH), BF16),
            pltpu.VMEM((1, WIDTH), jnp.int32),
            pltpu.VMEM((WIDTH, WIDTH), BF16),
            pltpu.VMEM((WIDTH, WIDTH), BF16),
            pltpu.VMEM((MODES, 1, WIDTH), F32),
            pltpu.VMEM((MODES, ny * span), F32),
            pltpu.VMEM((span, nu * LANES), BF16),
            pltpu.VMEM((WIDTH, WIDTH), BF16),
            pltpu.VMEM((WIDTH, WIDTH), BF16),
            pltpu.VMEM((WIDTH, WIDTH), BF16),
            pltpu.VMEM((WIDTH, WIDTH), BF16),
            pltpu.VMEM((3, CASES, WIDTH), F32),
            pltpu.VMEM((3, CASES, WIDTH), F32),
            pltpu.VMEM((8, WIDTH), F32),
            pltpu.VMEM((8, WIDTH), F32),
            pltpu.VMEM((32, WIDTH), F32),
            pltpu.VMEM((plane, 8, LANES), F32),
            pltpu.VMEM((plane, 8, LANES), F32),
            pltpu.VMEM((4, plane, 8, LANES), F32),
            pltpu.VMEM((plane * 8, GROUPS * LANES), F32),
            pltpu.VMEM((CHIPS_Z, 2, LANES), F32),
            pltpu.VMEM((2, CHIPS_Z, 8, LANES), F32),
            pltpu.VMEM((3, plane, 2, LANES), F32),
            pltpu.VMEM((3, plane, 8, LANES), F32),
            pltpu.VMEM((3, plane, 8, LANES), F32),
            pltpu.VMEM((3, 2, plane, 2, LANES), F32),
            pltpu.VMEM((CASES, WIDTH), F32),
            pltpu.VMEM((CASES, WIDTH), F32),
            pltpu.VMEM((CASES, WIDTH), F32),
            pltpu.VMEM((32, WIDTH), F32),
            pltpu.VMEM((16, LANES), F32),
            dma((6,)),
            dma((4, 4)),
            dma((4, 4)),
            dma,
            dma,
            dma((4,)),
            dma((4,)),
            dma((3,)),
            dma((3,)),
            dma((3,)),
            dma((3,)),
            dma((3, 2)),
            dma((3, 2)),
        ],
        compiler_params=pltpu.CompilerParams(
            collective_id=0, has_side_effects=True, vmem_limit_bytes=60 * 1024 * 1024
        ),
    )(
        loads[0],
        index_blocks,
        stiffness[0],
        dirichlet[0],
        jnp.transpose(modes, (1, 0, 2)),
        coarse,
    )
    return (alpha * search)[None], (projected - alpha * step)[None]


def solution(mesh):
    regions, nu = mesh.shape["region"], mesh.shape["sub"]
    nz = min(CHIPS_Z, regions // 2)
    both = ("region", "sub")
    return jax.shard_map(
        functools.partial(on_device, regions // nz, nz, nu),
        mesh=mesh,
        in_specs=(
            P(both, None, None),
            P(both, None),
            P(both, None, None),
            P(both, None, None),
            P(both, None, None),
            P(both, None),
        ),
        out_specs=(P(both, None, None), P(both, None, None)),
        check_vma=False,
    )
```
